128 devices in a mesh: lon: 16 (over z_hi, x, core), lat: 8 (over y, z_lo).
Axes of the slice: x: 4, y: 4, z: 4 (z_hi: 2, z_lo: 2; z = z_hi * 2 + z_lo), core: 2. Of those that a mesh axis runs over, the one named last changes fastest.
Arguments:
- weather: bfloat16 [2, 16, 2048, 512], P(None, 'lat', 'lon'), may hold values from -4 to 4
- windows: int32 [16], P('lat'), may hold values from 0 to 8, as said below
- window_table: int32 [16, 16], P('lat'), may hold values 0 or 1
- lon_gain: float32 [512], replicated, may hold values from 0.5 to 6, as said below
- lon_qkv: bfloat16 [512, 1536], replicated, may hold values from -0.25 to 0.25
- lon_out: bfloat16 [512, 512], replicated, may hold values from -1 to 1
- mer_gain: float32 [512], replicated, may hold values from 0.5 to 6, as said below
- mer_qkv: bfloat16 [512, 1536], replicated, may hold values from -0.25 to 0.25
- mer_out: bfloat16 [512, 512], replicated, may hold values from -0.5 to 0.5
- slopes: float32 [8], replicated, may hold values from 0.05 to 0.5
- mlp_gain: float32 [512], replicated, may hold values from 0.5 to 6, as said below
- mlp_in: bfloat16 [512, 2048], replicated, may hold values from -0.25 to 0.25
- mlp_out: bfloat16 [2048, 512], replicated, may hold values from -0.125 to 0.125
Outputs:
- updated: bfloat16 [2, 16, 2048, 512], P(None, 'lat', 'lon')
The draws below stay inside these ranges and needn't reach their ends.
Inputs may be any that keep to these rules, and one draw needn't show every extreme that they name: Latitude-dependent: rows nearest the poles have the widest windows, 8 blocks, rows near the equator narrow ones. `lon_gain`: Positive. `mer_gain`: Positive. `mlp_gain`: Positive.
All inputs are finite; a program needn't handle non-finite values. No bound on the sum of `window_table` on one device may be relied on, other than what follows from the above.
Results may differ from the reference program's by a relative error of at most 0.027.
The reference program's roundings to bfloat16 on the way count: a program that leaves them out, or rounds other values in their place, can miss the bound.
Values may be sent and summed in bfloat16 or wider, within the bound.
A program may use at most 128 MiB of HBM per device.

```python
import math
import jax
import jax.numpy as jnp
from jax import lax

CHANNELS = 512
HEADS = 8
HEAD_DIM = 64
FFN = 2048
BLOCK = 128
SAMPLES = 2
NLAT = 16
NLON = 2048
N_LON = 16


def spread_gain(key, low_value, high_value):
    exponent = jax.random.uniform(key, (CHANNELS,), jnp.float32, jnp.log(low_value), jnp.log(high_value))
    return jnp.exp(exponent)


def draw_windows(key, part):
    key = jax.random.fold_in(key, 5)
    row_ids = jnp.arange(NLAT, dtype=jnp.int32)
    polar = jnp.minimum(row_ids, NLAT - 1 - row_ids)
    half_rows = NLAT // 2
    base_width = N_LON // 2 * (half_rows - polar) // half_rows
    jitter = jax.random.randint(key, (NLAT,), 0, 2, dtype=jnp.int32)
    return jnp.clip(base_width + jitter, 0, N_LON // 2).astype(jnp.int32)


def draw_lon_gain(key, part):
    key = jax.random.fold_in(key, 11)
    return spread_gain(key, 0.5, 2.0)


def draw_mer_gain(key, part):
    key = jax.random.fold_in(key, 17)
    return spread_gain(key, 0.5, 2.0)


def draw_mlp_gain(key, part):
    key = jax.random.fold_in(key, 23)
    return spread_gain(key, 0.5, 2.0)


def plant(entries, stream_key, low, top_value):
    longest = entries.shape.index(max(entries.shape))
    spots = []
    for shift in (0, 1):
        where = [jax.random.randint(jax.random.fold_in(stream_key, axis), (), 0, length) for axis, length in enumerate(entries.shape)]
        where[longest] = (where[longest] + shift) % entries.shape[longest]
        spots.append(tuple(where))
    return entries.at[spots[0]].set(low).at[spots[1]].set(top_value)


def levels(own_key, dims, cuts, low, largest):
    factor_of = 1.0
    for dim, blocks in cuts:
        draws = jax.random.uniform(jax.random.fold_in(jax.random.fold_in(own_key, 6), dim), (blocks,), jnp.float32, low / len(cuts), largest / len(cuts))
        factor_of = factor_of * jnp.repeat(jnp.exp(draws), dims[dim] // blocks).reshape((-1,) + (1,) * (len(dims) - 1 - dim))
    return factor_of


def scatter_about(rng, dims, scale, bound, pieces=(), held_as=jnp.bfloat16):
    factor_of = levels(rng, dims, pieces, -0.22, 0.18) if pieces else 1.0
    drawn = jax.random.normal(rng, dims, jnp.float32) * scale * factor_of
    return jnp.minimum(jnp.maximum(drawn, -bound), bound).astype(held_as)


def setup_inputs(seed: int = 0) -> dict:
    keys = jax.random.split(jax.random.key(seed), 14)
    return {
        "weather": scatter_about(keys[0], (SAMPLES, NLAT, NLON, CHANNELS), 0.5, 4.0, ((1, 8), (2, 16))),
        "windows": draw_windows(jax.random.fold_in(keys[13], 71), 0),
        "window_table": plant((jax.random.randint(keys[2], (NLAT, N_LON), 0, 4) < 3).astype(jnp.int32), jax.random.fold_in(keys[2], 1), 0, 1),
        "lon_gain": draw_lon_gain(jax.random.fold_in(keys[13], 71), 0),
        "lon_qkv": scatter_about(keys[4], (CHANNELS, 3 * CHANNELS), CHANNELS ** -0.5, 0.25),
        "lon_out": scatter_about(keys[5], (CHANNELS, CHANNELS), (CHANNELS // 16) ** -0.5, 1.0),
        "mer_gain": draw_mer_gain(jax.random.fold_in(keys[13], 71), 0),
        "mer_qkv": scatter_about(keys[7], (CHANNELS, 3 * CHANNELS), CHANNELS ** -0.5, 0.25),
        "mer_out": scatter_about(keys[8], (CHANNELS, CHANNELS), (CHANNELS // 4) ** -0.5, 0.5),
        "slopes": jnp.clip(jnp.exp(jax.random.uniform(keys[9], (HEADS,), jnp.float32, math.log(0.05), math.log(0.5))), 0.05, 0.5),
        "mlp_gain": draw_mlp_gain(jax.random.fold_in(keys[13], 71), 0),
        "mlp_in": scatter_about(keys[11], (CHANNELS, FFN), CHANNELS ** -0.5, 0.25),
        "mlp_out": scatter_about(keys[12], (FFN, CHANNELS), FFN ** -0.5, 0.125),
    }


masked_score = -1e+30
norm_eps = 1e-06

def rms_scale(values_in, gain_row):
    widened = values_in.astype(jnp.float32)
    inverse = lax.rsqrt(lax.optimization_barrier(jnp.mean(widened * widened, axis=-1, keepdims=True)) + norm_eps)
    return (widened * inverse * gain_row).astype(jnp.bfloat16)

def project(values_in, weight):
    flattened = values_in.reshape(-1, values_in.shape[-1])
    product = jnp.dot(flattened, weight, preferred_element_type=jnp.float32)
    return product.reshape(values_in.shape[:-1] + (weight.shape[1],))

def lon_row(element, windows, window_table):
    cells_row, lat_row = element
    score_scale = 1.0 / math.sqrt(HEAD_DIM)
    widened = cells_row.astype(jnp.float32)
    queries = widened[:, 0]
    keys_row = widened[:, 1]
    values_row = widened[:, 2]
    scores = jnp.einsum('qhd,khd->hqk', queries, keys_row) * score_scale
    block_ids = jnp.arange(N_LON, dtype=jnp.int32)
    offset = (block_ids[None, :] - block_ids[:, None]) % N_LON
    reach_blocks = jnp.minimum(offset, N_LON - offset)
    table_row = window_table[lat_row]
    allowed = (reach_blocks <= windows[lat_row]) & ((offset == 0) | (table_row[offset] == 1))
    blocked = scores.reshape(HEADS, N_LON, BLOCK, N_LON, BLOCK)
    visible = allowed[None, :, None, :, None]
    peak_row = lax.optimization_barrier(jnp.max(jnp.where(visible, blocked, masked_score), axis=(3, 4), keepdims=True))
    weights = jnp.where(visible, jnp.exp(blocked - peak_row), 0.0)
    total_row = lax.optimization_barrier(jnp.sum(weights, axis=(3, 4))).reshape(HEADS, NLON, 1)
    rounded = lax.optimization_barrier(weights.astype(jnp.bfloat16)).astype(jnp.float32)
    rounded = rounded.reshape(HEADS, NLON, NLON)
    mixed = jnp.einsum('hqk,khd->qhd', rounded, values_row) / jnp.transpose(total_row, (1, 0, 2))
    return mixed.reshape(NLON, CHANNELS).astype(jnp.bfloat16)

def lon_attention(qkv_lon, windows, window_table):
    rows_all = qkv_lon.reshape(SAMPLES * NLAT, NLON, 3, HEADS, HEAD_DIM)
    row_lat = jnp.tile(jnp.arange(NLAT, dtype=jnp.int32), SAMPLES)
    outputs = lax.map(lambda element: lon_row(element, windows, window_table), (rows_all, row_lat))
    return outputs.reshape(SAMPLES, NLAT, NLON, CHANNELS)

def mer_attention(qkv_mer, slopes):
    half_cycle = NLON // 2
    score_scale = 1.0 / math.sqrt(HEAD_DIM)
    north = qkv_mer[:, :, :half_cycle]
    south = jnp.flip(qkv_mer[:, :, half_cycle:], axis=1)
    circle = jnp.concatenate([north, south], axis=1).astype(jnp.float32)
    circle = circle.reshape(SAMPLES, 2 * NLAT, half_cycle, 3, HEADS, HEAD_DIM)
    scores = jnp.einsum('bpchd,bschd->bchps', circle[:, :, :, 0], circle[:, :, :, 1]) * score_scale
    position = jnp.arange(2 * NLAT, dtype=jnp.int32)
    apart = jnp.abs(position[:, None] - position[None, :])
    distance = jnp.minimum(apart, 2 * NLAT - apart).astype(jnp.float32)
    scores = scores - slopes[None, None, :, None, None] * distance[None, None, None]
    peak_row = lax.optimization_barrier(jnp.max(scores, axis=-1, keepdims=True))
    weights = jnp.exp(scores - peak_row)
    total_row = lax.optimization_barrier(jnp.sum(weights, axis=-1, keepdims=True))
    rounded = lax.optimization_barrier(weights.astype(jnp.bfloat16)).astype(jnp.float32)
    mixed = jnp.einsum('bchps,bschd->bpchd', rounded, circle[:, :, :, 2])
    mixed = mixed / jnp.transpose(total_row, (0, 3, 1, 2, 4))
    mixed = mixed.reshape(SAMPLES, 2 * NLAT, half_cycle, CHANNELS).astype(jnp.bfloat16)
    north_out = mixed[:, :NLAT]
    south_out = jnp.flip(mixed[:, NLAT:], axis=1)
    return jnp.concatenate([north_out, south_out], axis=2)

def reference(weather, windows, window_table, lon_gain, lon_qkv, lon_out, mer_gain, mer_qkv, mer_out, slopes, mlp_gain, mlp_in, mlp_out):
    normed_lon = rms_scale(weather, lon_gain)
    qkv_lon = project(normed_lon, lon_qkv).astype(jnp.bfloat16)
    attn_lon = lon_attention(qkv_lon, windows, window_table)
    mixed_lon = (weather.astype(jnp.float32) + project(attn_lon, lon_out)).astype(jnp.bfloat16)
    normed_mer = rms_scale(mixed_lon, mer_gain)
    qkv_mer = project(normed_mer, mer_qkv).astype(jnp.bfloat16)
    attn_mer = mer_attention(qkv_mer, slopes)
    mixed_mer = (mixed_lon.astype(jnp.float32) + project(attn_mer, mer_out)).astype(jnp.bfloat16)
    normed_mlp = rms_scale(mixed_mer, mlp_gain)
    hidden = jax.nn.gelu(project(normed_mlp, mlp_in)).astype(jnp.bfloat16)
    return (mixed_mer.astype(jnp.float32) + project(hidden, mlp_out)).astype(jnp.bfloat16)
```

```python
import functools

import jax
import jax.numpy as jnp
from jax import lax
from jax.experimental import pallas as pl
from jax.experimental.pallas import tpu as pltpu
from jax.sharding import PartitionSpec as P

MESH = pl.DeviceIdType.MESH
F32 = jnp.float32
BF16 = jnp.bfloat16
BLOCK = 128
CH = 512
NEG = -1e30
EPS = 1e-06


def rms(x, gain):
    inv = lax.rsqrt(jnp.mean(x * x, axis=-1, keepdims=True) + EPS)
    return (x * inv * gain).astype(BF16)


def dot(a, b):
    return jnp.dot(a, b, preferred_element_type=F32)


def dot_nt(a, b):
    return lax.dot_general(a, b, (((1,), (1,)), ((), ())), preferred_element_type=F32)


def kernel(
    weather, windows, table, lon_gain, mer_gain, mlp_gain, slopes,
    lon_qkv_h, lon_out_h, mer_qkv_h, mer_out_h, mlp_in_h, mlp_out_h,
    out,
    rowx, kt, vaug, qs, attn, mixed, merx, xg, mqkv, outs, bias, dist,
    lon_qkv, lon_out, mer_qkv, mer_out, mlp_in, mlp_out,
    w_sem, l_sem, lon_ss, lon_rs, fwd_ss, fwd_rs, mer_ss, mer_rs, out_ss, out_rs,
):
    lo, band = lax.axis_index("lon"), lax.axis_index("lat")
    zh, x, c = lo // 8, (lo // 2) % 4, lo % 2
    y, zl = band // 2, band % 2
    base, r = (x // 2) * 2, x % 2
    s = (x // 2 + zh) % 2

    def dev(zh, x, c, y, zl):
        return ((zh * 4 + x) * 2 + c, y * 2 + zl)

    loads = [
        pltpu.make_async_copy(src, dst, w_sem.at[i])
        for i, (src, dst) in enumerate(
            [(lon_qkv_h, lon_qkv), (lon_out_h, lon_out), (mer_qkv_h, mer_qkv),
             (mer_out_h, mer_out), (mlp_in_h, mlp_in), (mlp_out_h, mlp_out)]
        )
    ]
    own_copy = pltpu.make_async_copy(weather.at[s, r], rowx.at[lo], l_sem.at[0])
    own_copy.start()
    loads[0].start()

    barrier = pltpu.get_barrier_semaphore()
    peers = [dev((zh + dz) % 2, (x + dx) % 4, c, y, zl) for dz in range(2) for dx in range(4) if dz + dx]
    peers.append(dev(zh, x, 1 - c, y, zl))
    lat_steps = [(dy, dl) for dy in range(4) for dl in range(2)]
    peers += [
        dev(zh, base + (r + dr) % 2, c, (y + dy) % 4, (zl + dl) % 2)
        for dr in range(2) for dy, dl in lat_steps if dr + dy + dl
    ]
    peers += [dev(1 - zh, x, c, (y + dy) % 4, (zl + dl) % 2) for dy, dl in lat_steps if dy + dl]
    for peer in peers:
        pl.semaphore_signal(barrier, inc=1, device_id=peer, device_id_type=MESH)
    pl.semaphore_wait(barrier, len(peers))

    def lon_copy(n):
        dz, dx = n // 4, n % 4
        tz, tx = (zh + dz) % 2, (x + dx) % 4
        return pltpu.make_async_remote_copy(
            src_ref=weather.at[(tx // 2 + tz) % 2, tx % 2],
            dst_ref=rowx.at[lo],
            send_sem=lon_ss.at[n],
            recv_sem=lon_rs.at[n],
            device_id=dev(tz, tx, c, y, zl),
            device_id_type=MESH,
        )

    def piece_of(n, core):
        dz, dx = n // 4, n % 4
        return (((zh + dz) % 2) * 4 + (x + 4 - dx) % 4) * 2 + core

    def fwd_copy(n):
        piece = piece_of(n, c)
        return pltpu.make_async_remote_copy(
            src_ref=rowx.at[piece],
            dst_ref=rowx.at[piece],
            send_sem=fwd_ss.at[n],
            recv_sem=fwd_rs.at[n],
            device_id=dev(zh, x, 1 - c, y, zl),
            device_id_type=MESH,
        )

    for n in (4, 6, 5, 7, 2, 1, 3):
        lon_copy(n).start()
    for load in loads[1:]:
        load.start()

    width = windows[r]
    row8 = lax.broadcasted_iota(jnp.int32, (8, BLOCK), 0)

    @pl.loop(0, 16)
    def _(kb):
        value = jnp.zeros((8, BLOCK), F32)
        for qi in range(4):
            qb = (qi // 2) * 8 + (base + qi % 2) * 2 + c
            d = (kb - qb + 16) % 16
            seen = (jnp.minimum(d, 16 - d) <= width) & ((d == 0) | (table[r, d] == 1))
            value = jnp.where(row8 == qi, jnp.where(seen, 0.0, NEG), value)
        bias[:, pl.ds(pl.multiple_of(kb * BLOCK, BLOCK), BLOCK)] = value

    def position(i):
        row, half = i // 16, (i // 8) % 2
        return jnp.where(half == 0, row, 31 - row)

    ii = lax.broadcasted_iota(jnp.int32, (256, 256), 0)
    jj = lax.broadcasted_iota(jnp.int32, (256, 256), 1)
    apart = jnp.abs(position(ii) - position(jj))
    apart = jnp.minimum(apart, 32 - apart).astype(F32)
    dist[...] = jnp.where(ii % 8 == jj % 8, apart, -1.0)

    loads[0].wait()
    low_half = lax.broadcasted_iota(jnp.int32, (BLOCK, BLOCK), 1) < 64
    one = jnp.ones((BLOCK, BLOCK), BF16)

    def keys_values(piece):
        normed = rms(rowx[piece].astype(F32), lon_gain[...])
        cells = pl.ds(pl.multiple_of(piece * BLOCK, BLOCK), BLOCK)
        k = dot(normed, lon_qkv[:, CH : 2 * CH])
        kt[:, :, cells] = k.T.astype(BF16).reshape(4, BLOCK, BLOCK)
        v = dot(normed, lon_qkv[:, 2 * CH :]).astype(BF16)
        for hp in range(4):
            part = v[:, hp * BLOCK : (hp + 1) * BLOCK]
            vaug[2 * hp, cells, :] = jnp.where(low_half, part, one)
            vaug[2 * hp + 1, cells, :] = jnp.where(low_half, one, part)

    @pl.loop(0, 9)
    def _(n):
        @pl.when(n == 0)
        def _():
            own_copy.wait()

        @pl.when((n > 0) & (n < 8))
        def _():
            lon_copy(n).wait_recv()

        @pl.when(n < 8)
        def _():
            fwd_copy(n).start()
            keys_values(piece_of(n, c))

        @pl.when(n > 0)
        def _():
            fwd_copy(n - 1).wait_recv()
            keys_values(piece_of(n - 1, 1 - c))

    def query_block(qi):
        return (qi // 2) * 8 + (base + qi % 2) * 2 + c

    for qi in range(4):
        normed = rms(rowx[query_block(qi)].astype(F32), lon_gain[...])
        q = dot(normed, lon_qkv[:, :CH]).astype(BF16) * jnp.bfloat16(0.125)
        for hp in range(4):
            qs[hp, qi * BLOCK : (qi + 1) * BLOCK, :] = q[:, hp * BLOCK : (hp + 1) * BLOCK]

    low_256 = lax.broadcasted_iota(jnp.int32, (256, BLOCK), 1) < 64
    none = jnp.zeros((256, BLOCK), BF16)

    @pl.loop(0, 8)
    def _(step):
        hp, qt = step // 2, step % 2
        rows = pl.ds(pl.multiple_of(qt * 256, 256), 256)
        qp = qs[hp, rows, :]
        half_bias = [bias[pl.ds(qt * 2 + j, 1), :] for j in range(2)]
        res = []
        for hh in range(2):
            qm = jnp.where(low_256, qp, none) if hh == 0 else jnp.where(low_256, none, qp)
            sc = dot(qm, kt[hp])
            sc = jnp.concatenate([sc[:BLOCK] + half_bias[0], sc[BLOCK:] + half_bias[1]], axis=0)
            m = jnp.max(sc, axis=-1, keepdims=True)
            p = jnp.exp(sc - m).astype(BF16)
            o = dot(p, vaug[2 * hp + hh])
            res.append(o / pltpu.roll(o, 64, 1))
        attn[rows, pl.ds(pl.multiple_of(hp * BLOCK, BLOCK), BLOCK)] = jnp.where(
            low_256, res[0], res[1]
        ).astype(BF16)

    loads[1].wait()
    for qi in range(4):
        new = dot(attn[qi * BLOCK : (qi + 1) * BLOCK, :], lon_out[...])
        mixed[qi // 2, qi % 2] = (rowx[query_block(qi)].astype(F32) + new).astype(BF16)

    def mer_copy(dr, dy, dl):
        tr, ty, tl = (r + dr) % 2, (y + dy) % 4, (zl + dl) % 2
        n = (dr * 4 + dy) * 2 + dl
        src = mixed.at[:, tr, pl.ds(pl.multiple_of((ty * 2 + tl) * 16, 16), 16), :]
        dst = merx.at[band * 2 + r]
        if n == 0:
            return pltpu.make_async_copy(src, dst, l_sem.at[1])
        return pltpu.make_async_remote_copy(
            src_ref=src, dst_ref=dst, send_sem=mer_ss.at[n], recv_sem=mer_rs.at[n],
            device_id=dev(zh, base + tr, c, ty, tl), device_id_type=MESH,
        )

    mer_steps = [(dr, dy, dl) for dr in range(2) for dy, dl in lat_steps]
    for step in mer_steps:
        mer_copy(*step).start()
    for load in loads[2:]:
        load.wait()
    for step in mer_steps:
        if sum(step):
            mer_copy(*step).wait_recv()
        else:
            mer_copy(*step).wait()

    cells = merx[...].astype(F32).reshape(32, 2, 8, CH)
    for g in range(2):
        part = cells[:, g].reshape(256, CH)
        xg[g * 256 : (g + 1) * 256, :] = part
        qkv = dot(rms(part, mer_gain[...]), mer_qkv[...]).astype(BF16)
        for j in range(12):
            mqkv[j, g * 256 : (g + 1) * 256, :] = qkv[:, j * BLOCK : (j + 1) * BLOCK]

    ones_256 = jnp.ones((256, BLOCK), BF16)

    @pl.loop(0, 4)
    def _(hp):
        far = dist[...]
        for g in range(2):
            rows = slice(g * 256, (g + 1) * 256)
            qp = mqkv[hp, rows, :] * jnp.bfloat16(0.125)
            kp = mqkv[4 + hp, rows, :]
            vp = mqkv[8 + hp, rows, :]
            res = []
            for hh in range(2):
                qm = jnp.where(low_256, qp, none) if hh == 0 else jnp.where(low_256, none, qp)
                vm = jnp.where(low_256, vp, ones_256) if hh == 0 else jnp.where(low_256, ones_256, vp)
                sc = dot_nt(qm, kp) - far * slopes[2 * hp + hh]
                sc = jnp.where(far >= 0.0, sc, NEG)
                m = jnp.max(sc, axis=-1, keepdims=True)
                p = jnp.exp(sc - m).astype(BF16)
                o = dot(p, vm)
                res.append(o / pltpu.roll(o, 64, 1))
            attn[rows, pl.ds(pl.multiple_of(hp * BLOCK, BLOCK), BLOCK)] = jnp.where(
                low_256, res[0], res[1]
            ).astype(BF16)

    parts = []
    for g in range(2):
        rows = slice(g * 256, (g + 1) * 256)
        mm = (xg[rows, :] + dot(attn[rows, :], mer_out[...])).astype(BF16).astype(F32)
        normed = rms(mm, mlp_gain[...])
        xg[rows, :] = mm
        attn[rows, :] = normed

    @pl.loop(0, 4)
    def _(j):
        cols = pl.ds(pl.multiple_of(j * CH, CH), CH)
        hidden = jax.nn.gelu(dot(attn[...], mlp_in[:, cols])).astype(BF16)
        xg[...] += dot(hidden, mlp_out[cols, :])

    done = jnp.swapaxes(xg[...].reshape(2, 32, 8, CH), 0, 1)
    outs[...] = done.reshape(16, 2, 16, CH).astype(BF16)

    def out_copy(dz, dy, dl):
        tz, ty, tl = (zh + dz) % 2, (y + dy) % 4, (zl + dl) % 2
        n = (dz * 4 + dy) * 2 + dl
        src = outs.at[pl.ds((ty * 2 + tl) * 2, 2), tz]
        dst = out.at[s, :, pl.ds(pl.multiple_of(band * 16, 16), 16), :]
        if n == 0:
            return pltpu.make_async_copy(src, dst, l_sem.at[2])
        return pltpu.make_async_remote_copy(
            src_ref=src, dst_ref=dst, send_sem=out_ss.at[n], recv_sem=out_rs.at[n],
            device_id=dev(tz, x, c, ty, tl), device_id_type=MESH,
        )

    for step in mer_steps:
        out_copy(*step).start()
    for n in range(1, 8):
        lon_copy(n).wait_send()
    for n in range(8):
        fwd_copy(n).wait_send()
    for step in mer_steps:
        if sum(step):
            mer_copy(*step).wait_send()
    for step in mer_steps:
        out_copy(*step).wait()


def per_device(
    weather, windows, window_table, lon_gain, lon_qkv, lon_out, mer_gain, mer_qkv, mer_out,
    slopes, mlp_gain, mlp_in, mlp_out,
):
    vmem = pl.BlockSpec(memory_space=pltpu.VMEM)
    smem = pl.BlockSpec(memory_space=pltpu.SMEM)
    hbm = pl.BlockSpec(memory_space=pl.ANY)
    dma = pltpu.SemaphoreType.DMA
    return pl.pallas_call(
        kernel,
        out_shape=jax.ShapeDtypeStruct(weather.shape, BF16),
        in_specs=[hbm, smem, smem, vmem, vmem, vmem, smem] + [hbm] * 6,
        out_specs=hbm,
        scratch_shapes=[
            pltpu.VMEM((16, BLOCK, CH), BF16),
            pltpu.VMEM((4, BLOCK, 2048), BF16),
            pltpu.VMEM((8, 2048, BLOCK), BF16),
            pltpu.VMEM((4, 512, BLOCK), BF16),
            pltpu.VMEM((512, CH), BF16),
            pltpu.VMEM((2, 2, BLOCK, CH), BF16),
            pltpu.VMEM((16, 2, 16, CH), BF16),
            pltpu.VMEM((512, CH), F32),
            pltpu.VMEM((12, 512, BLOCK), BF16),
            pltpu.VMEM((16, 2, 16, CH), BF16),
            pltpu.VMEM((8, 2048), F32),
            pltpu.VMEM((256, 256), F32),
            pltpu.VMEM((512, 1536), BF16),
            pltpu.VMEM((512, 512), BF16),
            pltpu.VMEM((512, 1536), BF16),
            pltpu.VMEM((512, 512), BF16),
            pltpu.VMEM((512, 2048), BF16),
            pltpu.VMEM((2048, 512), BF16),
            dma((6,)), dma((3,)),
            dma((8,)), dma((8,)), dma((8,)), dma((8,)),
            dma((16,)), dma((16,)), dma((16,)), dma((16,)),
        ],
        compiler_params=pltpu.CompilerParams(
            collective_id=0, has_side_effects=True, vmem_limit_bytes=56 * 1024 * 1024
        ),
        name="axial",
    )(
        weather, windows, window_table,
        lon_gain.reshape(1, CH), mer_gain.reshape(1, CH), mlp_gain.reshape(1, CH), slopes,
        lon_qkv, lon_out, mer_qkv, mer_out, mlp_in, mlp_out,
    )


def solution(mesh):
    return jax.shard_map(
        per_device,
        mesh=mesh,
        in_specs=(
            P(None, "lat", "lon", None), P("lat"), P("lat", None),
            P(), P(), P(), P(), P(), P(), P(), P(), P(), P(),
        ),
        out_specs=P(None, "lat", "lon", None),
        check_vma=False,
    )
```

```python
import functools

import jax
import jax.numpy as jnp
from jax import lax
from jax.experimental import pallas as pl
from jax.experimental.pallas import tpu as pltpu
from jax.sharding import PartitionSpec as P

MESH = pl.DeviceIdType.MESH
F32 = jnp.float32
BF16 = jnp.bfloat16
BLOCK = 128
CH = 512
NEG = -1e30
EPS = 1e-06


def rms(x, gain):
    inv = lax.rsqrt(jnp.mean(x * x, axis=-1, keepdims=True) + EPS)
    return (x * inv * gain).astype(BF16)


def dot(a, b):
    return jnp.dot(a, b, preferred_element_type=F32)


def dot_nt(a, b):
    return lax.dot_general(a, b, (((1,), (1,)), ((), ())), preferred_element_type=F32)


def kernel(
    weather, windows, table, lon_gain, mer_gain, mlp_gain, slopes,
    lon_qkv_h, lon_out_h, mer_qkv_h, mer_out_h, mlp_in_h, mlp_out_h,
    out,
    rowx, kt, vaug, qs, peak, accum, attn, mixed, merx, xg, mqkv, outs, bias, dist,
    lon_qkv, lon_out, mer_qkv, mer_out, mlp_in, mlp_out,
    w_sem, l_sem, lon_ss, lon_rs, fwd_ss, fwd_rs, mer_ss, mer_rs, out_ss, out_rs,
):
    lo, band = lax.axis_index("lon"), lax.axis_index("lat")
    zh, x, c = lo // 8, (lo // 2) % 4, lo % 2
    y, zl = band // 2, band % 2
    r = x % 2
    s = (x // 2 + zh) % 2

    def dev(zh, x, c, y, zl):
        return ((zh * 4 + x) * 2 + c, y * 2 + zl)

    def flip_x(e):
        return ((x // 2 + e // 2) % 2) * 2 + (x % 2 + e % 2) % 2

    loads = [
        pltpu.make_async_copy(src, dst, w_sem.at[i])
        for i, (src, dst) in enumerate(
            [(lon_qkv_h, lon_qkv), (lon_out_h, lon_out), (mer_qkv_h, mer_qkv),
             (mer_out_h, mer_out), (mlp_in_h, mlp_in), (mlp_out_h, mlp_out)]
        )
    ]
    own_copy = pltpu.make_async_copy(weather.at[s, r], rowx.at[0], l_sem.at[0])
    own_copy.start()
    loads[0].start()

    barrier = pltpu.get_barrier_semaphore()
    peers = [dev((zh + dz) % 2, flip_x(e), c, y, zl) for dz in range(2) for e in range(4) if dz + e]
    peers.append(dev(zh, x, 1 - c, y, zl))
    lat_steps = [(dy, dl) for dy in range(4) for dl in range(2)]
    peers += [
        dev(zh, flip_x(dr), c, (y + dy) % 4, (zl + dl) % 2)
        for dr in range(2) for dy, dl in lat_steps if dy + dl
    ]
    peers += [dev(1 - zh, x, c, (y + dy) % 4, (zl + dl) % 2) for dy, dl in lat_steps if dy + dl]
    for peer in peers:
        pl.semaphore_signal(barrier, inc=1, device_id=peer, device_id_type=MESH)
    pl.semaphore_wait(barrier, len(peers))

    def away(n):
        return (n // 2) % 2, n % 2 + 2 * (n // 4)

    def slot(n, handed):
        j = n // 2
        return (min(4 * j + 4, 14) if handed else max(4 * j - 2, 0)) + n % 2

    def lon_copy(n):
        dz, e = away(n)
        tz, tx = (zh + dz) % 2, flip_x(e)
        return pltpu.make_async_remote_copy(
            src_ref=weather.at[(tx // 2 + tz) % 2, tx % 2],
            dst_ref=rowx.at[slot(n, False)],
            send_sem=lon_ss.at[n],
            recv_sem=lon_rs.at[n],
            device_id=dev(tz, tx, c, y, zl),
            device_id_type=MESH,
        )

    def fwd_copy(n):
        return pltpu.make_async_remote_copy(
            src_ref=rowx.at[slot(n, False)],
            dst_ref=rowx.at[slot(n, True)],
            send_sem=fwd_ss.at[n],
            recv_sem=fwd_rs.at[n],
            device_id=dev(zh, x, 1 - c, y, zl),
            device_id_type=MESH,
        )

    for n in (2, 3, 1, 4, 5, 6, 7):
        lon_copy(n).start()
    own_copy.wait()
    fwd_copy(0).start()
    for load in loads[1:]:
        load.start()

    width = windows[r]
    rows_128 = lax.broadcasted_iota(jnp.int32, (BLOCK, BLOCK), 0)
    for n in range(8):
        for handed in range(2):
            dz, e = away(n)
            kb = ((zh + dz) % 2) * 8 + flip_x(e) * 2 + (c + handed) % 2
            value = jnp.zeros((BLOCK, BLOCK), F32)
            for qi in range(4):
                qb = ((zh + qi % 2) % 2) * 8 + flip_x(qi // 2) * 2 + c
                d = (kb - qb + 16) % 16
                seen = (jnp.minimum(d, 16 - d) <= width) & ((d == 0) | (table[r, d] == 1))
                value = jnp.where(rows_128 == qi, jnp.where(seen, 0.0, NEG), value)
            k0 = slot(n, handed) * BLOCK
            bias[:, k0 : k0 + BLOCK] = value.astype(BF16)

    def position(i):
        sl = i // 16
        row = (((y + sl // 4) % 4) * 2 + (zl + (sl // 2) % 2) % 2) * 2 + sl % 2
        half = ((i // 8) % 2 + zh) % 2
        return jnp.where(half == 0, row, 31 - row)

    ii = lax.broadcasted_iota(jnp.int32, (256, 256), 0)
    jj = lax.broadcasted_iota(jnp.int32, (256, 256), 1)
    apart = jnp.abs(position(ii) - position(jj))
    apart = jnp.minimum(apart, 32 - apart).astype(F32)
    dist[...] = jnp.where(ii % 8 == jj % 8, apart, -1.0)

    loads[0].wait()

    def keys_values(first, count):
        size = count * BLOCK
        normed = rms(rowx[first : first + count].reshape(size, CH).astype(F32), lon_gain[...])
        cells = slice(first * BLOCK, first * BLOCK + size)
        k = dot(normed, lon_qkv[:, CH : 2 * CH])
        kt[:, :, cells] = k.T.astype(BF16).reshape(4, BLOCK, size)
        v = dot(normed, lon_qkv[:, 2 * CH :]).astype(BF16)
        low = lax.broadcasted_iota(jnp.int32, (size, BLOCK), 1) < 64
        one = jnp.ones((size, BLOCK), BF16)
        for hp in range(4):
            part = v[:, hp * BLOCK : (hp + 1) * BLOCK]
            vaug[2 * hp, cells, :] = jnp.where(low, part, one)
            vaug[2 * hp + 1, cells, :] = jnp.where(low, one, part)
        return normed

    def queries(normed, dz):
        q = dot(normed, lon_qkv[:, :CH]).astype(BF16) * jnp.bfloat16(0.125)
        for e in range(2):
            for hp in range(4):
                r0 = (e * 2 + dz) * BLOCK
                qs[hp, r0 : r0 + BLOCK, :] = q[e * BLOCK : (e + 1) * BLOCK, hp * BLOCK : (hp + 1) * BLOCK]

    def attend(r0, size, first, count, begin=False, end=False):
        rows = slice(r0, r0 + size)
        cells = slice(first * BLOCK, (first + count) * BLOCK)
        low = lax.broadcasted_iota(jnp.int32, (size, BLOCK), 1) < 64
        none = jnp.zeros((size, BLOCK), BF16)
        block = lax.broadcasted_iota(jnp.int32, (size, BLOCK), 0) // BLOCK + r0 // BLOCK
        lane = lax.broadcasted_iota(jnp.int32, (size, BLOCK), 1)
        hot = jnp.where(block == lane, 1.0, 0.0).astype(BF16)

        @pl.loop(0, 4)
        def _(hp):
            qp = qs[hp, rows, :]
            kp = jnp.concatenate([kt[hp, :, cells], bias[:, cells]], axis=0)
            scores = [
                dot(jnp.concatenate([qm, hot], axis=1), kp)
                for qm in (jnp.where(low, qp, none), jnp.where(low, none, qp))
            ]
            res = []
            for hh in range(2):
                h = 2 * hp + hh
                m = jnp.max(scores[hh], axis=-1, keepdims=True)
                if not begin:
                    old = peak[h, rows, :][:, :1]
                    m = jnp.maximum(old, m)
                p = jnp.exp(scores[hh] - m).astype(BF16)
                o = dot(p, vaug[h, cells, :])
                if not begin:
                    o = accum[h, rows, :] * jnp.exp(old - m) + o
                if end:
                    res.append(o / pltpu.roll(o, 64, 1))
                else:
                    accum[h, rows, :] = o
                    peak[h, rows, :] = jnp.broadcast_to(m, (size, BLOCK))
            if end:
                attn[rows, pl.ds(pl.multiple_of(hp * BLOCK, BLOCK), BLOCK)] = jnp.where(
                    low, res[0], res[1]
                ).astype(BF16)

    lon_copy(1).wait_recv()
    fwd_copy(1).start()
    queries(keys_values(0, 2), 0)
    for n in (2, 3):
        lon_copy(n).wait_recv()
        fwd_copy(n).start()
    queries(keys_values(2, 2), 1)
    for n in (0, 1):
        fwd_copy(n).wait_recv()
    keys_values(4, 2)
    attend(0, 512, 0, 6, begin=True)
    for j in (2, 3):
        for n in (2 * j, 2 * j + 1):
            lon_copy(n).wait_recv()
            fwd_copy(n).start()
        for n in (2 * j - 2, 2 * j - 1):
            fwd_copy(n).wait_recv()
        keys_values(4 * j - 2, 4)
        attend(0, 512, 4 * j - 2, 4)
    for n in (6, 7):
        fwd_copy(n).wait_recv()
    keys_values(14, 2)
    loads[1].wait()

    def mer_copy(dr, dy, dl):
        ty, tl = (y + dy) % 4, (zl + dl) % 2
        n = (dr * 4 + dy) * 2 + dl
        src = mixed.at[dr, :, pl.ds(pl.multiple_of((ty * 2 + tl) * 16, 16), 16), :]
        dst = merx.at[(((4 - dy) % 4) * 2 + dl) * 2 + r]
        if n == 0:
            return pltpu.make_async_copy(src, dst, l_sem.at[1])
        return pltpu.make_async_remote_copy(
            src_ref=src, dst_ref=dst, send_sem=mer_ss.at[n], recv_sem=mer_rs.at[n],
            device_id=dev(zh, flip_x(dr), c, ty, tl), device_id_type=MESH,
        )

    mer_steps = [(dr, dy, dl) for dr in range(2) for dy, dl in lat_steps]
    for e in (1, 0):
        attend(e * 256, 256, 14, 2, end=True)
        new = dot(attn[e * 256 : (e + 1) * 256, :], lon_out[...])
        for dz in range(2):
            part = rowx[2 * dz + e].astype(F32) + new[dz * BLOCK : (dz + 1) * BLOCK]
            mixed[e, dz] = part.astype(BF16)
        for dy, dl in lat_steps[::-1]:
            mer_copy(e, dy, dl).start()
    for load in loads[2:]:
        load.wait()
    for step in mer_steps:
        if sum(step):
            mer_copy(*step).wait_recv()
        else:
            mer_copy(*step).wait()

    low_256 = lax.broadcasted_iota(jnp.int32, (256, BLOCK), 1) < 64
    none = jnp.zeros((256, BLOCK), BF16)
    cells = merx[...].astype(F32).reshape(32, 2, 8, CH)
    for g in range(2):
        part = cells[:, g].reshape(256, CH)
        xg[g * 256 : (g + 1) * 256, :] = part
        qkv = dot(rms(part, mer_gain[...]), mer_qkv[...]).astype(BF16)
        for j in range(12):
            mqkv[j, g * 256 : (g + 1) * 256, :] = qkv[:, j * BLOCK : (j + 1) * BLOCK]

    ones_256 = jnp.ones((256, BLOCK), BF16)

    @pl.loop(0, 4)
    def _(hp):
        far = dist[...]
        units = [(g, hh) for g in range(2) for hh in range(2)]
        scores = []
        for g, hh in units:
            rows = slice(g * 256, (g + 1) * 256)
            qp = mqkv[hp, rows, :] * jnp.bfloat16(0.125)
            qm = jnp.where(low_256, qp, none) if hh == 0 else jnp.where(low_256, none, qp)
            scores.append(dot_nt(qm, mqkv[4 + hp, rows, :]))
        res = []
        for (g, hh), sc in zip(units, scores):
            vp = mqkv[8 + hp, g * 256 : (g + 1) * 256, :]
            vm = jnp.where(low_256, vp, ones_256) if hh == 0 else jnp.where(low_256, ones_256, vp)
            sc = jnp.where(far >= 0.0, sc - far * slopes[2 * hp + hh], NEG)
            m = jnp.max(sc, axis=-1, keepdims=True)
            p = jnp.exp(sc - m).astype(BF16)
            o = dot(p, vm)
            res.append(o / pltpu.roll(o, 64, 1))
        for g in range(2):
            attn[g * 256 : (g + 1) * 256, pl.ds(pl.multiple_of(hp * BLOCK, BLOCK), BLOCK)] = jnp.where(
                low_256, res[2 * g], res[2 * g + 1]
            ).astype(BF16)

    for g in range(2):
        rows = slice(g * 256, (g + 1) * 256)
        mm = (xg[rows, :] + dot(attn[rows, :], mer_out[...])).astype(BF16).astype(F32)
        normed = rms(mm, mlp_gain[...])
        xg[rows, :] = mm
        attn[rows, :] = normed

    @pl.loop(0, 4)
    def _(j):
        cols = pl.ds(pl.multiple_of(j * CH, CH), CH)
        hidden = jax.nn.gelu(dot(attn[...], mlp_in[:, cols])).astype(BF16)
        xg[...] += dot(hidden, mlp_out[cols, :])

    done = jnp.swapaxes(xg[...].reshape(2, 32, 8, CH), 0, 1)
    outs[...] = done.reshape(16, 2, 16, CH).astype(BF16)

    def out_copy(dz, dy, dl):
        tz, ty, tl = (zh + dz) % 2, (y + dy) % 4, (zl + dl) % 2
        n = (dz * 4 + dy) * 2 + dl
        src = outs.at[pl.ds((dy * 2 + dl) * 2, 2), dz]
        dst = out.at[s, :, pl.ds(pl.multiple_of(band * 16, 16), 16), :]
        if n == 0:
            return pltpu.make_async_copy(src, dst, l_sem.at[2])
        return pltpu.make_async_remote_copy(
            src_ref=src, dst_ref=dst, send_sem=out_ss.at[n], recv_sem=out_rs.at[n],
            device_id=dev(tz, x, c, ty, tl), device_id_type=MESH,
        )

    for step in mer_steps:
        out_copy(*step).start()
    for n in range(1, 8):
        lon_copy(n).wait_send()
    for n in range(8):
        fwd_copy(n).wait_send()
    for step in mer_steps:
        if sum(step):
            mer_copy(*step).wait_send()
    for step in mer_steps:
        out_copy(*step).wait()


def per_device(
    weather, windows, window_table, lon_gain, lon_qkv, lon_out, mer_gain, mer_qkv, mer_out,
    slopes, mlp_gain, mlp_in, mlp_out,
):
    vmem = pl.BlockSpec(memory_space=pltpu.VMEM)
    smem = pl.BlockSpec(memory_space=pltpu.SMEM)
    hbm = pl.BlockSpec(memory_space=pl.ANY)
    dma = pltpu.SemaphoreType.DMA
    return pl.pallas_call(
        kernel,
        out_shape=jax.ShapeDtypeStruct(weather.shape, BF16),
        in_specs=[hbm, smem, smem, vmem, vmem, vmem, smem] + [hbm] * 6,
        out_specs=hbm,
        scratch_shapes=[
            pltpu.VMEM((16, BLOCK, CH), BF16),
            pltpu.VMEM((4, BLOCK, 2048), BF16),
            pltpu.VMEM((8, 2048, BLOCK), BF16),
            pltpu.VMEM((4, 512, BLOCK), BF16),
            pltpu.VMEM((8, 512, BLOCK), F32),
            pltpu.VMEM((8, 512, BLOCK), F32),
            pltpu.VMEM((512, CH), BF16),
            pltpu.VMEM((2, 2, BLOCK, CH), BF16),
            pltpu.VMEM((16, 2, 16, CH), BF16),
            pltpu.VMEM((512, CH), F32),
            pltpu.VMEM((12, 512, BLOCK), BF16),
            pltpu.VMEM((16, 2, 16, CH), BF16),
            pltpu.VMEM((BLOCK, 2048), BF16),
            pltpu.VMEM((256, 256), F32),
            pltpu.VMEM((512, 1536), BF16),
            pltpu.VMEM((512, 512), BF16),
            pltpu.VMEM((512, 1536), BF16),
            pltpu.VMEM((512, 512), BF16),
            pltpu.VMEM((512, 2048), BF16),
            pltpu.VMEM((2048, 512), BF16),
            dma((6,)), dma((3,)),
            dma((8,)), dma((8,)), dma((8,)), dma((8,)),
            dma((16,)), dma((16,)), dma((16,)), dma((16,)),
        ],
        compiler_params=pltpu.CompilerParams(
            collective_id=0, has_side_effects=True, vmem_limit_bytes=56 * 1024 * 1024
        ),
        name="axial",
    )(
        weather, windows, window_table,
        lon_gain.reshape(1, CH), mer_gain.reshape(1, CH), mlp_gain.reshape(1, CH), slopes,
        lon_qkv, lon_out, mer_qkv, mer_out, mlp_in, mlp_out,
    )


def solution(mesh):
    return jax.shard_map(
        per_device,
        mesh=mesh,
        in_specs=(
            P(None, "lat", "lon", None), P("lat"), P("lat", None),
            P(), P(), P(), P(), P(), P(), P(), P(), P(), P(),
        ),
        out_specs=P(None, "lat", "lon", None),
        check_vma=False,
    )
```

```python
import functools

import jax
import jax.numpy as jnp
from jax import lax
from jax.experimental import pallas as pl
from jax.experimental.pallas import tpu as pltpu
from jax.sharding import PartitionSpec as P

MESH = pl.DeviceIdType.MESH
F32 = jnp.float32
BF16 = jnp.bfloat16
BLOCK = 128
CH = 512
NEG = -1e30
EPS = 1e-06


def rms(x, gain):
    inv = lax.rsqrt(jnp.mean(x * x, axis=-1, keepdims=True) + EPS)
    return (x * inv * gain).astype(BF16)


def dot(a, b):
    return jnp.dot(a, b, preferred_element_type=F32)


def dot_nt(a, b):
    return lax.dot_general(a, b, (((1,), (1,)), ((), ())), preferred_element_type=F32)


def kernel(
    weather, windows, table, lon_gain, mer_gain, mlp_gain, slopes,
    lon_qkv_h, lon_out_h, mer_qkv_h, mer_out_h, mlp_in_h, mlp_out_h,
    out,
    rowx, kt, vaug, qs, peak, accum, attn, mixed, merx, xg, mqkv, outs, bias, dist,
    lon_qkv, lon_out, mer_qkv, mer_out, mlp_in, mlp_out,
    w_sem, l_sem, lon_ss, lon_rs, fwd_ss, fwd_rs, mer_ss, mer_rs, out_ss, out_rs,
):
    lo, band = lax.axis_index("lon"), lax.axis_index("lat")
    zh, x, c = lo // 8, (lo // 2) % 4, lo % 2
    y, zl = band // 2, band % 2
    r = x % 2
    s = (x // 2 + zh) % 2

    def dev(zh, x, c, y, zl):
        return ((zh * 4 + x) * 2 + c, y * 2 + zl)

    def flip_x(e):
        return ((x // 2 + e // 2) % 2) * 2 + (x % 2 + e % 2) % 2

    loads = [
        pltpu.make_async_copy(src, dst, w_sem.at[i])
        for i, (src, dst) in enumerate(
            [(lon_qkv_h, lon_qkv), (lon_out_h, lon_out), (mer_qkv_h, mer_qkv),
             (mer_out_h, mer_out), (mlp_in_h, mlp_in), (mlp_out_h, mlp_out)]
        )
    ]
    own_copy = pltpu.make_async_copy(weather.at[s, r], rowx.at[0], l_sem.at[0])
    own_copy.start()
    loads[0].start()

    barrier = pltpu.get_barrier_semaphore()
    peers = [dev((zh + dz) % 2, flip_x(e), c, y, zl) for dz in range(2) for e in range(4) if dz + e]
    peers.append(dev(zh, x, 1 - c, y, zl))
    lat_steps = [(dy, dl) for dy in range(4) for dl in range(2)]
    peers += [
        dev(zh, flip_x(dr), c, (y + dy) % 4, (zl + dl) % 2)
        for dr in range(2) for dy, dl in lat_steps if dy + dl
    ]
    peers += [dev(1 - zh, x, c, (y + dy) % 4, (zl + dl) % 2) for dy, dl in lat_steps if dy + dl]
    for peer in peers:
        pl.semaphore_signal(barrier, inc=1, device_id=peer, device_id_type=MESH)
    pl.semaphore_wait(barrier, len(peers))

    def away(n):
        return (n // 2) % 2, n % 2 + 2 * (n // 4)

    def slot(n, handed):
        j = n // 2
        return (min(4 * j + 4, 14) if handed else max(4 * j - 2, 0)) + n % 2

    def lon_copy(n):
        dz, e = away(n)
        tz, tx = (zh + dz) % 2, flip_x(e)
        return pltpu.make_async_remote_copy(
            src_ref=weather.at[(tx // 2 + tz) % 2, tx % 2],
            dst_ref=rowx.at[slot(n, False)],
            send_sem=lon_ss.at[n],
            recv_sem=lon_rs.at[n],
            device_id=dev(tz, tx, c, y, zl),
            device_id_type=MESH,
        )

    def fwd_copy(n):
        return pltpu.make_async_remote_copy(
            src_ref=rowx.at[slot(n, False)],
            dst_ref=rowx.at[slot(n, True)],
            send_sem=fwd_ss.at[n],
            recv_sem=fwd_rs.at[n],
            device_id=dev(zh, x, 1 - c, y, zl),
            device_id_type=MESH,
        )

    for n in (2, 1, 3, 5):
        lon_copy(n).start()
    own_copy.wait()
    fwd_copy(0).start()
    for load in loads[1:]:
        load.start()

    width = windows[r]
    rows_128 = lax.broadcasted_iota(jnp.int32, (BLOCK, BLOCK), 0)
    for n in range(8):
        for handed in range(2):
            dz, e = away(n)
            kb = ((zh + dz) % 2) * 8 + flip_x(e) * 2 + (c + handed) % 2
            value = jnp.zeros((BLOCK, BLOCK), F32)
            for qi in range(4):
                qb = ((zh + qi % 2) % 2) * 8 + flip_x(qi // 2) * 2 + c
                d = (kb - qb + 16) % 16
                seen = (jnp.minimum(d, 16 - d) <= width) & ((d == 0) | (table[r, d] == 1))
                value = jnp.where(rows_128 == qi, jnp.where(seen, 0.0, NEG), value)
            k0 = slot(n, handed) * BLOCK
            bias[:, k0 : k0 + BLOCK] = value.astype(BF16)

    def position(i):
        sl = i // 16
        row = (((y + sl // 4) % 4) * 2 + (zl + (sl // 2) % 2) % 2) * 2 + sl % 2
        half = ((i // 8) % 2 + zh) % 2
        return jnp.where(half == 0, row, 31 - row)

    ii = lax.broadcasted_iota(jnp.int32, (256, 256), 0)
    jj = lax.broadcasted_iota(jnp.int32, (256, 256), 1)
    apart = jnp.abs(position(ii) - position(jj))
    apart = jnp.minimum(apart, 32 - apart).astype(F32)
    dist[...] = jnp.where(ii % 8 == jj % 8, apart, -1.0)

    loads[0].wait()

    def keys_values(first, count):
        size = count * BLOCK
        normed = rms(rowx[first : first + count].reshape(size, CH).astype(F32), lon_gain[...])
        cells = slice(first * BLOCK, first * BLOCK + size)
        k = dot(normed, lon_qkv[:, CH : 2 * CH])
        kt[:, :, cells] = k.T.astype(BF16).reshape(4, BLOCK, size)
        v = dot(normed, lon_qkv[:, 2 * CH :]).astype(BF16)
        low = lax.broadcasted_iota(jnp.int32, (size, BLOCK), 1) < 64
        one = jnp.ones((size, BLOCK), BF16)
        for hp in range(4):
            part = v[:, hp * BLOCK : (hp + 1) * BLOCK]
            vaug[2 * hp, cells, :] = jnp.where(low, part, one)
            vaug[2 * hp + 1, cells, :] = jnp.where(low, one, part)
        return normed

    def queries(normed, dz):
        q = dot(normed, lon_qkv[:, :CH]).astype(BF16) * jnp.bfloat16(0.125)
        for e in range(2):
            for hp in range(4):
                r0 = (e * 2 + dz) * BLOCK
                qs[hp, r0 : r0 + BLOCK, :] = q[e * BLOCK : (e + 1) * BLOCK, hp * BLOCK : (hp + 1) * BLOCK]

    def attend(r0, size, first, count, heads, begin=False, end=False):
        rows = slice(r0, r0 + size)
        cells = slice(first * BLOCK, (first + count) * BLOCK)
        low = lax.broadcasted_iota(jnp.int32, (size, BLOCK), 1) < 64
        none = jnp.zeros((size, BLOCK), BF16)
        block = lax.broadcasted_iota(jnp.int32, (size, BLOCK), 0) // BLOCK + r0 // BLOCK
        lane = lax.broadcasted_iota(jnp.int32, (size, BLOCK), 1)
        hot = jnp.where(block == lane, 1.0, 0.0).astype(BF16)

        def score(hp, hh):
            qp = qs[hp, rows, :]
            qm = jnp.where(low, none, qp) if hh else jnp.where(low, qp, none)
            kp = jnp.concatenate([kt[hp, :, cells], bias[:, cells]], axis=0)
            return dot(jnp.concatenate([qm, hot], axis=1), kp)

        @pl.loop(heads[0], heads[1], step=2)
        def _(pair):
            units = [(pair + j, hh) for j in range(2) for hh in range(2)]
            ahead = score(*units[0])
            res = []
            for i, (hp, hh) in enumerate(units):
                sc = ahead
                if i + 1 < len(units):
                    ahead = score(*units[i + 1])
                h = 2 * hp + hh
                m = jnp.max(sc, axis=-1, keepdims=True)
                if begin:
                    p = jnp.exp(sc - m).astype(BF16)
                    o = dot(p, vaug[h, cells, :])
                else:
                    old = peak[h, rows, :]
                    m = jnp.maximum(old, m)
                    p = [jnp.exp(sc[:, j * BLOCK : (j + 1) * BLOCK] - m).astype(BF16) for j in range(count)]
                    o = dot(jnp.concatenate(p, axis=1), vaug[h, cells, :])
                    o = accum[h, rows, :] * jnp.exp(old - m) + o
                if end:
                    res.append(o / pltpu.roll(o, 64, 1))
                    if hh:
                        attn[rows, pl.ds(pl.multiple_of(hp * BLOCK, BLOCK), BLOCK)] = jnp.where(
                            low, res[-2], res[-1]
                        ).astype(BF16)
                else:
                    accum[h, rows, :] = o
                    peak[h, rows, :] = jnp.broadcast_to(m, (size, BLOCK))

    lon_copy(1).wait_recv()
    fwd_copy(1).start()
    queries(keys_values(0, 2), 0)
    for n in (1, 2):
        lon_copy(n).wait_send()
    for n in (4, 7, 6):
        lon_copy(n).start()
    lon_copy(2).wait_recv()
    fwd_copy(2).start()
    for n in (0, 1):
        fwd_copy(n).wait_recv()
    keys_values(4, 2)
    lon_copy(3).wait_recv()
    fwd_copy(3).start()
    queries(keys_values(2, 2), 1)
    attend(0, 512, 0, 6, (0, 2), begin=True)
    lon_copy(5).wait_recv()
    fwd_copy(5).start()
    attend(0, 512, 0, 6, (2, 4), begin=True)
    lon_copy(4).wait_recv()
    fwd_copy(4).start()
    for n in (2, 3):
        fwd_copy(n).wait_recv()
    keys_values(6, 4)
    attend(0, 512, 6, 4, (0, 4))
    for n in (6, 7):
        lon_copy(n).wait_recv()
        fwd_copy(n).start()
    for n in (4, 5):
        fwd_copy(n).wait_recv()
    keys_values(10, 4)
    for n in (6, 7):
        fwd_copy(n).wait_recv()
    keys_values(14, 2)
    loads[1].wait()

    def mer_copy(dr, dy, dl):
        ty, tl = (y + dy) % 4, (zl + dl) % 2
        n = (dr * 4 + dy) * 2 + dl
        src = mixed.at[dr, :, pl.ds(pl.multiple_of((ty * 2 + tl) * 16, 16), 16), :]
        dst = merx.at[(((4 - dy) % 4) * 2 + dl) * 2 + r]
        if n == 0:
            return pltpu.make_async_copy(src, dst, l_sem.at[1])
        return pltpu.make_async_remote_copy(
            src_ref=src, dst_ref=dst, send_sem=mer_ss.at[n], recv_sem=mer_rs.at[n],
            device_id=dev(zh, flip_x(dr), c, ty, tl), device_id_type=MESH,
        )

    mer_steps = [(dr, dy, dl) for dr in range(2) for dy, dl in lat_steps]
    for e in (1, 0):
        attend(e * 256, 256, 10, 6, (0, 4), end=True)
        new = dot(attn[e * 256 : (e + 1) * 256, :], lon_out[...])
        for dz in range(2):
            part = rowx[2 * dz + e].astype(F32) + new[dz * BLOCK : (dz + 1) * BLOCK]
            mixed[e, dz] = part.astype(BF16)
        for dy, dl in lat_steps[::-1]:
            mer_copy(e, dy, dl).start()
    for load in loads[2:]:
        load.wait()
    for step in mer_steps:
        if sum(step):
            mer_copy(*step).wait_recv()
        else:
            mer_copy(*step).wait()

    low_256 = lax.broadcasted_iota(jnp.int32, (256, BLOCK), 1) < 64
    none = jnp.zeros((256, BLOCK), BF16)
    cells = merx[...].astype(F32).reshape(32, 2, 8, CH)
    for g in range(2):
        part = cells[:, g].reshape(256, CH)
        xg[g * 256 : (g + 1) * 256, :] = part
        qkv = dot(rms(part, mer_gain[...]), mer_qkv[...]).astype(BF16)
        for j in range(12):
            mqkv[j, g * 256 : (g + 1) * 256, :] = qkv[:, j * BLOCK : (j + 1) * BLOCK]

    ones_256 = jnp.ones((256, BLOCK), BF16)

    @pl.loop(0, 4)
    def _(hp):
        far = dist[...]
        units = [(g, hh) for g in range(2) for hh in range(2)]
        scores = []
        for g, hh in units:
            rows = slice(g * 256, (g + 1) * 256)
            qp = mqkv[hp, rows, :] * jnp.bfloat16(0.125)
            qm = jnp.where(low_256, qp, none) if hh == 0 else jnp.where(low_256, none, qp)
            scores.append(dot_nt(qm, mqkv[4 + hp, rows, :]))
        res = []
        for (g, hh), sc in zip(units, scores):
            vp = mqkv[8 + hp, g * 256 : (g + 1) * 256, :]
            vm = jnp.where(low_256, vp, ones_256) if hh == 0 else jnp.where(low_256, ones_256, vp)
            sc = jnp.where(far >= 0.0, sc - far * slopes[2 * hp + hh], NEG)
            m = jnp.max(sc, axis=-1, keepdims=True)
            p = jnp.exp(sc - m).astype(BF16)
            o = dot(p, vm)
            res.append(o / pltpu.roll(o, 64, 1))
        for g in range(2):
            attn[g * 256 : (g + 1) * 256, pl.ds(pl.multiple_of(hp * BLOCK, BLOCK), BLOCK)] = jnp.where(
                low_256, res[2 * g], res[2 * g + 1]
            ).astype(BF16)

    for g in range(2):
        rows = slice(g * 256, (g + 1) * 256)
        mm = (xg[rows, :] + dot(attn[rows, :], mer_out[...])).astype(BF16).astype(F32)
        normed = rms(mm, mlp_gain[...])
        xg[rows, :] = mm
        attn[rows, :] = normed

    @pl.loop(0, 4)
    def _(j):
        cols = pl.ds(pl.multiple_of(j * CH, CH), CH)
        hidden = jax.nn.gelu(dot(attn[...], mlp_in[:, cols])).astype(BF16)
        xg[...] += dot(hidden, mlp_out[cols, :])

    done = jnp.swapaxes(xg[...].reshape(2, 32, 8, CH), 0, 1)
    outs[...] = done.reshape(16, 2, 16, CH).astype(BF16)

    def out_copy(dz, dy, dl):
        tz, ty, tl = (zh + dz) % 2, (y + dy) % 4, (zl + dl) % 2
        n = (dz * 4 + dy) * 2 + dl
        src = outs.at[pl.ds((dy * 2 + dl) * 2, 2), dz]
        dst = out.at[s, :, pl.ds(pl.multiple_of(band * 16, 16), 16), :]
        if n == 0:
            return pltpu.make_async_copy(src, dst, l_sem.at[2])
        return pltpu.make_async_remote_copy(
            src_ref=src, dst_ref=dst, send_sem=out_ss.at[n], recv_sem=out_rs.at[n],
            device_id=dev(tz, x, c, ty, tl), device_id_type=MESH,
        )

    for step in mer_steps:
        out_copy(*step).start()
    for n in (3, 4, 5, 6, 7):
        lon_copy(n).wait_send()
    for n in range(8):
        fwd_copy(n).wait_send()
    for step in mer_steps:
        if sum(step):
            mer_copy(*step).wait_send()
    for step in mer_steps:
        out_copy(*step).wait()


def per_device(
    weather, windows, window_table, lon_gain, lon_qkv, lon_out, mer_gain, mer_qkv, mer_out,
    slopes, mlp_gain, mlp_in, mlp_out,
):
    vmem = pl.BlockSpec(memory_space=pltpu.VMEM)
    smem = pl.BlockSpec(memory_space=pltpu.SMEM)
    hbm = pl.BlockSpec(memory_space=pl.ANY)
    dma = pltpu.SemaphoreType.DMA
    return pl.pallas_call(
        kernel,
        out_shape=jax.ShapeDtypeStruct(weather.shape, BF16),
        in_specs=[hbm, smem, smem, vmem, vmem, vmem, smem] + [hbm] * 6,
        out_specs=hbm,
        scratch_shapes=[
            pltpu.VMEM((16, BLOCK, CH), BF16),
            pltpu.VMEM((4, BLOCK, 2048), BF16),
            pltpu.VMEM((8, 2048, BLOCK), BF16),
            pltpu.VMEM((4, 512, BLOCK), BF16),
            pltpu.VMEM((8, 512, BLOCK), F32),
            pltpu.VMEM((8, 512, BLOCK), F32),
            pltpu.VMEM((512, CH), BF16),
            pltpu.VMEM((2, 2, BLOCK, CH), BF16),
            pltpu.VMEM((16, 2, 16, CH), BF16),
            pltpu.VMEM((512, CH), F32),
            pltpu.VMEM((12, 512, BLOCK), BF16),
            pltpu.VMEM((16, 2, 16, CH), BF16),
            pltpu.VMEM((BLOCK, 2048), BF16),
            pltpu.VMEM((256, 256), F32),
            pltpu.VMEM((512, 1536), BF16),
            pltpu.VMEM((512, 512), BF16),
            pltpu.VMEM((512, 1536), BF16),
            pltpu.VMEM((512, 512), BF16),
            pltpu.VMEM((512, 2048), BF16),
            pltpu.VMEM((2048, 512), BF16),
            dma((6,)), dma((3,)),
            dma((8,)), dma((8,)), dma((8,)), dma((8,)),
            dma((16,)), dma((16,)), dma((16,)), dma((16,)),
        ],
        compiler_params=pltpu.CompilerParams(
            collective_id=0, has_side_effects=True, vmem_limit_bytes=56 * 1024 * 1024
        ),
        name="axial",
    )(
        weather, windows, window_table,
        lon_gain.reshape(1, CH), mer_gain.reshape(1, CH), mlp_gain.reshape(1, CH), slopes,
        lon_qkv, lon_out, mer_qkv, mer_out, mlp_in, mlp_out,
    )


def solution(mesh):
    return jax.shard_map(
        per_device,
        mesh=mesh,
        in_specs=(
            P(None, "lat", "lon", None), P("lat"), P("lat", None),
            P(), P(), P(), P(), P(), P(), P(), P(), P(), P(),
        ),
        out_specs=P(None, "lat", "lon", None),
        check_vma=False,
    )
```

```python
import functools

import jax
import jax.numpy as jnp
from jax import lax
from jax.experimental import pallas as pl
from jax.experimental.pallas import tpu as pltpu
from jax.sharding import PartitionSpec as P

MESH = pl.DeviceIdType.MESH
F32 = jnp.float32
BF16 = jnp.bfloat16
BLOCK = 128
CH = 512
NEG = -1e30
EPS = 1e-06


def rms(x, gain):
    inv = lax.rsqrt(jnp.mean(x * x, axis=-1, keepdims=True) + EPS)
    return (x * inv * gain).astype(BF16)


def dot(a, b):
    return jnp.dot(a, b, preferred_element_type=F32)


def dot_nt(a, b):
    return lax.dot_general(a, b, (((1,), (1,)), ((), ())), preferred_element_type=F32)


def kernel(
    weather, windows, table, lon_gain, mer_gain, mlp_gain, slopes,
    lon_qkv_h, lon_out_h, mer_qkv_h, mer_out_h, mlp_in_h, mlp_out_h,
    out,
    rowx, kt, vaug, qs, peak, accum, attn, mixed, merx, xg, mqkv, outs, bias, dist,
    lon_qkv, lon_out, mer_qkv, mer_out, mlp_in, mlp_out,
    w_sem, l_sem, lon_ss, lon_rs, fwd_ss, fwd_rs, mer_ss, mer_rs, out_ss, out_rs,
):
    lo, band = lax.axis_index("lon"), lax.axis_index("lat")
    zh, x, c = lo // 8, (lo // 2) % 4, lo % 2
    y, zl = band // 2, band % 2
    r = x % 2
    s = (x // 2 + zh) % 2

    def dev(zh, x, c, y, zl):
        return ((zh * 4 + x) * 2 + c, y * 2 + zl)

    def flip_x(e):
        return ((x // 2 + e // 2) % 2) * 2 + (x % 2 + e % 2) % 2

    loads = [
        pltpu.make_async_copy(src, dst, w_sem.at[i])
        for i, (src, dst) in enumerate(
            [(lon_qkv_h, lon_qkv), (lon_out_h, lon_out), (mer_qkv_h, mer_qkv),
             (mer_out_h, mer_out), (mlp_in_h, mlp_in), (mlp_out_h, mlp_out)]
        )
    ]
    own_copy = pltpu.make_async_copy(weather.at[s, r], rowx.at[0], l_sem.at[0])
    own_copy.start()
    loads[0].start()

    barrier = pltpu.get_barrier_semaphore()
    peers = [dev((zh + dz) % 2, flip_x(e), c, y, zl) for dz in range(2) for e in range(4) if dz + e]
    peers.append(dev(zh, x, 1 - c, y, zl))
    lat_steps = [(dy, dl) for dy in range(4) for dl in range(2)]
    peers += [
        dev(zh, flip_x(dr), c, (y + dy) % 4, (zl + dl) % 2)
        for dr in range(2) for dy, dl in lat_steps if dy + dl
    ]
    peers += [dev(1 - zh, x, c, (y + dy) % 4, (zl + dl) % 2) for dy, dl in lat_steps if dy + dl]
    for peer in peers:
        pl.semaphore_signal(barrier, inc=1, device_id=peer, device_id_type=MESH)
    pl.semaphore_wait(barrier, len(peers))

    def away(n):
        return (n // 2) % 2, n % 2 + 2 * (n // 4)

    def slot(n, handed):
        j = n // 2
        return (min(4 * j + 4, 14) if handed else max(4 * j - 2, 0)) + n % 2

    def lon_copy(n):
        dz, e = away(n)
        tz, tx = (zh + dz) % 2, flip_x(e)
        return pltpu.make_async_remote_copy(
            src_ref=weather.at[(tx // 2 + tz) % 2, tx % 2],
            dst_ref=rowx.at[slot(n, False)],
            send_sem=lon_ss.at[n],
            recv_sem=lon_rs.at[n],
            device_id=dev(tz, tx, c, y, zl),
            device_id_type=MESH,
        )

    def fwd_copy(n):
        return pltpu.make_async_remote_copy(
            src_ref=rowx.at[slot(n, False)],
            dst_ref=rowx.at[slot(n, True)],
            send_sem=fwd_ss.at[n],
            recv_sem=fwd_rs.at[n],
            device_id=dev(zh, x, 1 - c, y, zl),
            device_id_type=MESH,
        )

    for n in (2, 1, 3, 5):
        lon_copy(n).start()
    own_copy.wait()
    fwd_copy(0).start()
    for load in loads[1:]:
        load.start()

    width = windows[r]
    rows_128 = lax.broadcasted_iota(jnp.int32, (BLOCK, BLOCK), 0)
    for n in range(8):
        for handed in range(2):
            dz, e = away(n)
            kb = ((zh + dz) % 2) * 8 + flip_x(e) * 2 + (c + handed) % 2
            value = jnp.zeros((BLOCK, BLOCK), F32)
            for qi in range(4):
                qb = ((zh + qi % 2) % 2) * 8 + flip_x(qi // 2) * 2 + c
                d = (kb - qb + 16) % 16
                seen = (jnp.minimum(d, 16 - d) <= width) & ((d == 0) | (table[r, d] == 1))
                value = jnp.where(rows_128 == qi, jnp.where(seen, 0.0, NEG), value)
            k0 = slot(n, handed) * BLOCK
            bias[:, k0 : k0 + BLOCK] = value.astype(BF16)

    def piece_at(dr, dy, dl):
        near = 0 if dy in (1, 2) else 1
        return near * 8 + dr * 4 + ((dy - 1 - 2 * near) % 4) * 2 + dl

    def position(i):
        near, dr, dyi, dl = i // 128, (i // 64) % 2, (i // 32) % 2, (i // 16) % 2
        row = (((y + 1 + 2 * near + dyi) % 4) * 2 + (zl + dl) % 2) * 2 + (r + dr) % 2
        half = ((i // 8) % 2 + zh) % 2
        return jnp.where(half == 0, row, 31 - row)

    ii = lax.broadcasted_iota(jnp.int32, (256, 256), 0)
    jj = lax.broadcasted_iota(jnp.int32, (256, 256), 1)
    apart = jnp.abs(position(ii) - position(jj))
    apart = jnp.minimum(apart, 32 - apart).astype(F32)
    dist[...] = jnp.where(ii % 8 == jj % 8, apart, -1.0)

    loads[0].wait()

    def keys_values(first, count):
        size = count * BLOCK
        normed = rms(rowx[first : first + count].reshape(size, CH).astype(F32), lon_gain[...])
        cells = slice(first * BLOCK, first * BLOCK + size)
        k = dot(normed, lon_qkv[:, CH : 2 * CH])
        kt[:, :, cells] = k.T.astype(BF16).reshape(4, BLOCK, size)
        v = dot(normed, lon_qkv[:, 2 * CH :]).astype(BF16)
        low = lax.broadcasted_iota(jnp.int32, (size, BLOCK), 1) < 64
        one = jnp.ones((size, BLOCK), BF16)
        for hp in range(4):
            part = v[:, hp * BLOCK : (hp + 1) * BLOCK]
            vaug[2 * hp, cells, :] = jnp.where(low, part, one)
            vaug[2 * hp + 1, cells, :] = jnp.where(low, one, part)
        return normed

    def queries(normed, dz):
        q = dot(normed, lon_qkv[:, :CH]).astype(BF16) * jnp.bfloat16(0.125)
        for e in range(2):
            for hp in range(4):
                r0 = (e * 2 + dz) * BLOCK
                qs[hp, r0 : r0 + BLOCK, :] = q[e * BLOCK : (e + 1) * BLOCK, hp * BLOCK : (hp + 1) * BLOCK]

    def attend(r0, size, first, count, heads, begin=False, end=False):
        rows = slice(r0, r0 + size)
        cells = slice(first * BLOCK, (first + count) * BLOCK)
        low = lax.broadcasted_iota(jnp.int32, (size, BLOCK), 1) < 64
        none = jnp.zeros((size, BLOCK), BF16)
        block = lax.broadcasted_iota(jnp.int32, (size, BLOCK), 0) // BLOCK + r0 // BLOCK
        lane = lax.broadcasted_iota(jnp.int32, (size, BLOCK), 1)
        hot = jnp.where(block == lane, 1.0, 0.0).astype(BF16)

        def score(hp, hh):
            qp = qs[hp, rows, :]
            qm = jnp.where(low, none, qp) if hh else jnp.where(low, qp, none)
            kp = jnp.concatenate([kt[hp, :, cells], bias[:, cells]], axis=0)
            return dot(jnp.concatenate([qm, hot], axis=1), kp)

        @pl.loop(heads[0], heads[1], step=2)
        def _(pair):
            units = [(pair + j, hh) for j in range(2) for hh in range(2)]
            ahead = score(*units[0])
            res = []
            for i, (hp, hh) in enumerate(units):
                sc = ahead
                if i + 1 < len(units):
                    ahead = score(*units[i + 1])
                h = 2 * hp + hh
                m = jnp.max(sc, axis=-1, keepdims=True)
                if begin:
                    p = jnp.exp(sc - m).astype(BF16)
                    o = dot(p, vaug[h, cells, :])
                else:
                    old = peak[h, rows, :]
                    m = jnp.maximum(old, m)
                    p = [jnp.exp(sc[:, j * BLOCK : (j + 1) * BLOCK] - m).astype(BF16) for j in range(count)]
                    o = dot(jnp.concatenate(p, axis=1), vaug[h, cells, :])
                    o = accum[h, rows, :] * jnp.exp(old - m) + o
                if end:
                    res.append(o / pltpu.roll(o, 64, 1))
                    if hh:
                        attn[rows, pl.ds(pl.multiple_of(hp * BLOCK, BLOCK), BLOCK)] = jnp.where(
                            low, res[-2], res[-1]
                        ).astype(BF16)
                else:
                    accum[h, rows, :] = o
                    peak[h, rows, :] = jnp.broadcast_to(m, (size, BLOCK))

    lon_copy(1).wait_recv()
    fwd_copy(1).start()
    queries(keys_values(0, 2), 0)
    for n in (1, 2):
        lon_copy(n).wait_send()
    for n in (4, 7, 6):
        lon_copy(n).start()
    lon_copy(2).wait_recv()
    fwd_copy(2).start()
    for n in (0, 1):
        fwd_copy(n).wait_recv()
    keys_values(4, 2)
    lon_copy(3).wait_recv()
    fwd_copy(3).start()
    queries(keys_values(2, 2), 1)
    attend(0, 512, 0, 6, (0, 2), begin=True)
    lon_copy(5).wait_recv()
    fwd_copy(5).start()
    lon_copy(4).wait_recv()
    fwd_copy(4).start()
    attend(0, 512, 0, 6, (2, 4), begin=True)
    for n in (2, 3):
        fwd_copy(n).wait_recv()
    keys_values(6, 4)
    attend(0, 512, 6, 4, (0, 2))
    for n in (6, 7):
        lon_copy(n).wait_recv()
        fwd_copy(n).start()
    attend(0, 512, 6, 4, (2, 4))
    for n in (4, 5):
        fwd_copy(n).wait_recv()
    keys_values(10, 4)
    for n in (6, 7):
        fwd_copy(n).wait_recv()
    keys_values(14, 2)
    loads[1].wait()

    def mer_copy(dr, dy, dl):
        ty, tl = (y + dy) % 4, (zl + dl) % 2
        n = (dr * 4 + dy) * 2 + dl
        src = mixed.at[dr, :, pl.ds(pl.multiple_of((ty * 2 + tl) * 16, 16), 16), :]
        dst = merx.at[piece_at(dr, (4 - dy) % 4, dl)]
        if n == 0:
            return pltpu.make_async_copy(src, dst, l_sem.at[1])
        return pltpu.make_async_remote_copy(
            src_ref=src, dst_ref=dst, send_sem=mer_ss.at[n], recv_sem=mer_rs.at[n],
            device_id=dev(zh, flip_x(dr), c, ty, tl), device_id_type=MESH,
        )

    mer_steps = [(dr, dy, dl) for dr in range(2) for dy, dl in lat_steps]
    for e in (1, 0):
        attend(e * 256, 256, 10, 6, (0, 4), end=True)
        new = dot(attn[e * 256 : (e + 1) * 256, :], lon_out[...])
        for dz in range(2):
            part = rowx[2 * dz + e].astype(F32) + new[dz * BLOCK : (dz + 1) * BLOCK]
            mixed[e, dz] = part.astype(BF16)
        for dy, dl in lat_steps[::-1]:
            mer_copy(e, dy, dl).start()
    for load in loads[2:]:
        load.wait()
    for dr in (1, 0):
        for dy, dl in lat_steps:
            if dr + dy + dl:
                mer_copy(dr, dy, dl).wait_recv()
            else:
                mer_copy(dr, dy, dl).wait()
        parts = [[], []]
        for near in range(2):
            p0 = near * 8 + dr * 4
            cells = merx[p0 : p0 + 4].astype(F32).reshape(8, 2, 8, CH)
            for g in range(2):
                parts[g].append(cells[:, g].reshape(64, CH))
        cells = jnp.concatenate(parts[0] + parts[1], axis=0)
        qkv = dot(rms(cells, mer_gain[...]), mer_qkv[...]).astype(BF16)
        for q in range(4):
            r0 = (q // 2) * 256 + (q % 2) * 128 + dr * 64
            xg[r0 : r0 + 64, :] = cells[q * 64 : (q + 1) * 64]
            for j in range(12):
                mqkv[j, r0 : r0 + 64, :] = qkv[q * 64 : (q + 1) * 64, j * BLOCK : (j + 1) * BLOCK]

    low_256 = lax.broadcasted_iota(jnp.int32, (256, BLOCK), 1) < 64
    none = jnp.zeros((256, BLOCK), BF16)
    ones_256 = jnp.ones((256, BLOCK), BF16)

    @pl.loop(0, 4)
    def _(hp):
        far = dist[...]
        units = [(hp, g, hh) for g in range(2) for hh in range(2)]

        def score(hp, g, hh):
            rows = slice(g * 256, (g + 1) * 256)
            qp = mqkv[hp, rows, :] * jnp.bfloat16(0.125)
            return dot_nt(jnp.where(low_256, none, qp) if hh else jnp.where(low_256, qp, none), mqkv[4 + hp, rows, :])

        ahead = [score(*units[0]), score(*units[1])]
        res = []
        for i, (hp, g, hh) in enumerate(units):
            sc = ahead.pop(0)
            if i + 2 < len(units):
                ahead.append(score(*units[i + 2]))
            rows = slice(g * 256, (g + 1) * 256)
            vp = mqkv[8 + hp, rows, :]
            vm = jnp.where(low_256, ones_256, vp) if hh else jnp.where(low_256, vp, ones_256)
            sc = jnp.where(far >= 0.0, sc - far * slopes[2 * hp + hh], NEG)
            m = jnp.max(sc, axis=-1, keepdims=True)
            p = jnp.exp(sc - m).astype(BF16)
            o = dot(p, vm)
            res.append(o / pltpu.roll(o, 64, 1))
            if hh:
                attn[rows, pl.ds(pl.multiple_of(hp * BLOCK, BLOCK), BLOCK)] = jnp.where(
                    low_256, res[-2], res[-1]
                ).astype(BF16)

    def out_copy(dz, dy, dl):
        tz, ty, tl = (zh + dz) % 2, (y + dy) % 4, (zl + dl) % 2
        n = (dz * 4 + dy) * 2 + dl
        piece = piece_at(0, dy, dl)
        src = outs.at[piece // 8, :, piece % 4, dz]
        dst = out.at[s, :, pl.ds(pl.multiple_of(band * 16, 16), 16), :]
        if n == 0:
            return pltpu.make_async_copy(src, dst, l_sem.at[2])
        return pltpu.make_async_remote_copy(
            src_ref=src, dst_ref=dst, send_sem=out_ss.at[n], recv_sem=out_rs.at[n],
            device_id=dev(tz, x, c, ty, tl), device_id_type=MESH,
        )

    for near in range(2):
        halves = []
        for g in range(2):
            r0 = g * 256 + near * 128
            halves.append(xg[r0 : r0 + 128, :] + dot(attn[r0 : r0 + 128, :], mer_out[...]))
        mm = jnp.concatenate([h.reshape(16, 1, 8, CH) for h in halves], axis=1).reshape(256, CH)
        mm = mm.astype(BF16).astype(F32)
        normed = rms(mm, mlp_gain[...])

        def up(j):
            return dot(normed, mlp_in[:, j * CH : (j + 1) * CH])

        ahead = up(0)
        for j in range(4):
            hidden = ahead
            if j < 3:
                ahead = up(j + 1)
            mm = mm + dot(jax.nn.gelu(hidden).astype(BF16), mlp_out[j * CH : (j + 1) * CH, :])
        mm = mm.astype(BF16).reshape(2, 4, 2, 16, CH)
        for dr in range(2):
            outs[near, (r + dr) % 2] = mm[dr]
        for dy in ((2, 1), (3, 0))[near]:
            for dz in (1, 0):
                for dl in (1, 0):
                    out_copy(dz, dy, dl).start()

    for n in (3, 4, 5, 6, 7):
        lon_copy(n).wait_send()
    for n in range(8):
        fwd_copy(n).wait_send()
    for step in mer_steps:
        if sum(step):
            mer_copy(*step).wait_send()
    for step in mer_steps:
        out_copy(*step).wait()


def per_device(
    weather, windows, window_table, lon_gain, lon_qkv, lon_out, mer_gain, mer_qkv, mer_out,
    slopes, mlp_gain, mlp_in, mlp_out,
):
    vmem = pl.BlockSpec(memory_space=pltpu.VMEM)
    smem = pl.BlockSpec(memory_space=pltpu.SMEM)
    hbm = pl.BlockSpec(memory_space=pl.ANY)
    dma = pltpu.SemaphoreType.DMA
    return pl.pallas_call(
        kernel,
        out_shape=jax.ShapeDtypeStruct(weather.shape, BF16),
        in_specs=[hbm, smem, smem, vmem, vmem, vmem, smem] + [hbm] * 6,
        out_specs=hbm,
        scratch_shapes=[
            pltpu.VMEM((16, BLOCK, CH), BF16),
            pltpu.VMEM((4, BLOCK, 2048), BF16),
            pltpu.VMEM((8, 2048, BLOCK), BF16),
            pltpu.VMEM((4, 512, BLOCK), BF16),
            pltpu.VMEM((8, 512, BLOCK), F32),
            pltpu.VMEM((8, 512, BLOCK), F32),
            pltpu.VMEM((512, CH), BF16),
            pltpu.VMEM((2, 2, BLOCK, CH), BF16),
            pltpu.VMEM((16, 2, 16, CH), BF16),
            pltpu.VMEM((512, CH), F32),
            pltpu.VMEM((12, 512, BLOCK), BF16),
            pltpu.VMEM((2, 2, 4, 2, 16, CH), BF16),
            pltpu.VMEM((BLOCK, 2048), BF16),
            pltpu.VMEM((256, 256), F32),
            pltpu.VMEM((512, 1536), BF16),
            pltpu.VMEM((512, 512), BF16),
            pltpu.VMEM((512, 1536), BF16),
            pltpu.VMEM((512, 512), BF16),
            pltpu.VMEM((512, 2048), BF16),
            pltpu.VMEM((2048, 512), BF16),
            dma((6,)), dma((3,)),
            dma((8,)), dma((8,)), dma((8,)), dma((8,)),
            dma((16,)), dma((16,)), dma((16,)), dma((16,)),
        ],
        compiler_params=pltpu.CompilerParams(
            collective_id=0, has_side_effects=True, vmem_limit_bytes=56 * 1024 * 1024
        ),
        name="axial",
    )(
        weather, windows, window_table,
        lon_gain.reshape(1, CH), mer_gain.reshape(1, CH), mlp_gain.reshape(1, CH), slopes,
        lon_qkv, lon_out, mer_qkv, mer_out, mlp_in, mlp_out,
    )


def solution(mesh):
    return jax.shard_map(
        per_device,
        mesh=mesh,
        in_specs=(
            P(None, "lat", "lon", None), P("lat"), P("lat", None),
            P(), P(), P(), P(), P(), P(), P(), P(), P(), P(),
        ),
        out_specs=P(None, "lat", "lon", None),
        check_vma=False,
    )
```

```python
import functools

import jax
import jax.numpy as jnp
from jax import lax
from jax.experimental import pallas as pl
from jax.experimental.pallas import tpu as pltpu
from jax.sharding import PartitionSpec as P

MESH = pl.DeviceIdType.MESH
F32 = jnp.float32
BF16 = jnp.bfloat16
BLOCK = 128
CH = 512
NEG = -1e30
EPS = 1e-06


def rms(x, gain):
    inv = lax.rsqrt(jnp.mean(x * x, axis=-1, keepdims=True) + EPS)
    return (x * inv * gain).astype(BF16)


def dot(a, b):
    return jnp.dot(a, b, preferred_element_type=F32)


def dot_nt(a, b):
    return lax.dot_general(a, b, (((1,), (1,)), ((), ())), preferred_element_type=F32)


def kernel(
    weather, windows, table, lon_gain, mer_gain, mlp_gain, slopes,
    lon_qkv_h, lon_out_h, mer_qkv_h, mer_out_h, mlp_in_h, mlp_out_h,
    out,
    rowx, kt, vaug, qs, peak, accum, attn, mixed, merx, xg, mqkv, outs, bias, dist,
    lon_qkv, lon_out, mer_qkv, mer_out, mlp_in, mlp_out,
    w_sem, l_sem, lon_ss, lon_rs, fwd_ss, fwd_rs, mer_ss, mer_rs, out_ss, out_rs,
):
    lo, band = lax.axis_index("lon"), lax.axis_index("lat")
    zh, x, c = lo // 8, (lo // 2) % 4, lo % 2
    y, zl = band // 2, band % 2
    r = x % 2
    s = (x // 2 + zh) % 2

    def dev(zh, x, c, y, zl):
        return ((zh * 4 + x) * 2 + c, y * 2 + zl)

    def flip_x(e):
        return ((x // 2 + e // 2) % 2) * 2 + (x % 2 + e % 2) % 2

    loads = [
        pltpu.make_async_copy(src, dst, w_sem.at[i])
        for i, (src, dst) in enumerate(
            [(lon_qkv_h, lon_qkv), (lon_out_h, lon_out), (mer_qkv_h, mer_qkv),
             (mer_out_h, mer_out), (mlp_in_h, mlp_in), (mlp_out_h, mlp_out)]
        )
    ]
    own_copy = pltpu.make_async_copy(weather.at[s, r], rowx.at[0], l_sem.at[0])
    own_copy.start()
    loads[0].start()

    barrier = pltpu.get_barrier_semaphore()
    peers = [dev((zh + dz) % 2, flip_x(e), c, y, zl) for dz in range(2) for e in range(4) if dz + e]
    peers.append(dev(zh, x, 1 - c, y, zl))
    lat_steps = [(dy, dl) for dy in range(4) for dl in range(2)]
    peers += [
        dev(zh, flip_x(dr), c, (y + dy) % 4, (zl + dl) % 2)
        for dr in range(2) for dy, dl in lat_steps if dy + dl
    ]
    peers += [dev(1 - zh, x, c, (y + dy) % 4, (zl + dl) % 2) for dy, dl in lat_steps if dy + dl]
    for peer in peers:
        pl.semaphore_signal(barrier, inc=1, device_id=peer, device_id_type=MESH)
    pl.semaphore_wait(barrier, len(peers))

    def away(n):
        return (n // 2) % 2, n % 2 + 2 * (n // 4)

    def slot(n, handed):
        return ((4, 8, 10, 14) if handed else (0, 2, 6, 12))[n // 2] + n % 2

    def lon_copy(n):
        dz, e = away(n)
        tz, tx = (zh + dz) % 2, flip_x(e)
        return pltpu.make_async_remote_copy(
            src_ref=weather.at[(tx // 2 + tz) % 2, tx % 2],
            dst_ref=rowx.at[slot(n, False)],
            send_sem=lon_ss.at[n],
            recv_sem=lon_rs.at[n],
            device_id=dev(tz, tx, c, y, zl),
            device_id_type=MESH,
        )

    def fwd_copy(n):
        return pltpu.make_async_remote_copy(
            src_ref=rowx.at[slot(n, False)],
            dst_ref=rowx.at[slot(n, True)],
            send_sem=fwd_ss.at[n],
            recv_sem=fwd_rs.at[n],
            device_id=dev(zh, x, 1 - c, y, zl),
            device_id_type=MESH,
        )

    for n in (2, 1, 3, 5):
        lon_copy(n).start()
    own_copy.wait()
    fwd_copy(0).start()
    for load in loads[1:]:
        load.start()

    width = windows[r]
    rows_128 = lax.broadcasted_iota(jnp.int32, (BLOCK, BLOCK), 0)
    for n in range(8):
        for handed in range(2):
            dz, e = away(n)
            kb = ((zh + dz) % 2) * 8 + flip_x(e) * 2 + (c + handed) % 2
            value = jnp.zeros((BLOCK, BLOCK), F32)
            for qi in range(4):
                qb = ((zh + qi % 2) % 2) * 8 + flip_x(qi // 2) * 2 + c
                d = (kb - qb + 16) % 16
                seen = (jnp.minimum(d, 16 - d) <= width) & ((d == 0) | (table[r, d] == 1))
                value = jnp.where(rows_128 == qi, jnp.where(seen, 0.0, NEG), value)
            k0 = slot(n, handed) * BLOCK
            bias[:, k0 : k0 + BLOCK] = value.astype(BF16)

    def piece_at(dr, dy, dl):
        near = 0 if dy in (1, 2) else 1
        return near * 8 + dr * 4 + ((dy - 1 - 2 * near) % 4) * 2 + dl

    def position(i):
        near, dr, dyi, dl = i // 128, (i // 64) % 2, (i // 32) % 2, (i // 16) % 2
        row = (((y + 1 + 2 * near + dyi) % 4) * 2 + (zl + dl) % 2) * 2 + (r + dr) % 2
        half = ((i // 8) % 2 + zh) % 2
        return jnp.where(half == 0, row, 31 - row)

    ii = lax.broadcasted_iota(jnp.int32, (256, 256), 0)
    jj = lax.broadcasted_iota(jnp.int32, (256, 256), 1)
    apart = jnp.abs(position(ii) - position(jj))
    apart = jnp.minimum(apart, 32 - apart).astype(F32)
    dist[...] = jnp.where(ii % 8 == jj % 8, apart, -1.0)

    loads[0].wait()

    def keys_values(first, count):
        size = count * BLOCK
        normed = rms(rowx[first : first + count].reshape(size, CH).astype(F32), lon_gain[...])
        cells = slice(first * BLOCK, first * BLOCK + size)
        k = dot(normed, lon_qkv[:, CH : 2 * CH])
        kt[:, :, cells] = k.T.astype(BF16).reshape(4, BLOCK, size)
        v = dot(normed, lon_qkv[:, 2 * CH :]).astype(BF16)
        low = lax.broadcasted_iota(jnp.int32, (size, BLOCK), 1) < 64
        one = jnp.ones((size, BLOCK), BF16)
        for hp in range(4):
            part = v[:, hp * BLOCK : (hp + 1) * BLOCK]
            vaug[2 * hp, cells, :] = jnp.where(low, part, one)
            vaug[2 * hp + 1, cells, :] = jnp.where(low, one, part)
        return normed

    def queries(normed, dz):
        q = dot(normed, lon_qkv[:, :CH]).astype(BF16) * jnp.bfloat16(0.125)
        for e in range(2):
            for hp in range(4):
                r0 = (e * 2 + dz) * BLOCK
                qs[hp, r0 : r0 + BLOCK, :] = q[e * BLOCK : (e + 1) * BLOCK, hp * BLOCK : (hp + 1) * BLOCK]

    def attend(r0, size, first, count, heads, begin=False, end=False):
        rows = slice(r0, r0 + size)
        cells = slice(first * BLOCK, (first + count) * BLOCK)
        low = lax.broadcasted_iota(jnp.int32, (size, BLOCK), 1) < 64
        none = jnp.zeros((size, BLOCK), BF16)
        block = lax.broadcasted_iota(jnp.int32, (size, BLOCK), 0) // BLOCK + r0 // BLOCK
        lane = lax.broadcasted_iota(jnp.int32, (size, BLOCK), 1)
        hot = jnp.where(block == lane, 1.0, 0.0).astype(BF16)

        def score(hp, hh):
            qp = qs[hp, rows, :]
            qms = [jnp.where(low, qp, none), jnp.where(low, none, qp)]
            kp = jnp.concatenate([kt[hp, :, cells], bias[:, cells]], axis=0)
            if not end:
                return dot(jnp.concatenate([qms[hh], hot], axis=1), kp)
            if hh == 0:
                both = jnp.concatenate([jnp.concatenate([qm, hot], axis=1) for qm in qms], axis=0)
                stacked.append(dot(both, kp))
            return stacked[-1][hh * size : (hh + 1) * size]

        stacked = []

        @pl.loop(heads[0], heads[1], step=2)
        def _(pair):
            units = [(pair + j, hh) for j in range(2) for hh in range(2)]
            ahead = score(*units[0])
            res = []
            for i, (hp, hh) in enumerate(units):
                sc = ahead
                if i + 1 < len(units):
                    ahead = score(*units[i + 1])
                h = 2 * hp + hh
                m = jnp.max(sc, axis=-1, keepdims=True)
                if begin:
                    p = jnp.exp(sc - m).astype(BF16)
                    o = dot(p, vaug[h, cells, :])
                else:
                    old = peak[h, rows, :]
                    m = jnp.maximum(old, m)
                    p = [jnp.exp(sc[:, j * BLOCK : (j + 1) * BLOCK] - m).astype(BF16) for j in range(count)]
                    o = dot(jnp.concatenate(p, axis=1), vaug[h, cells, :])
                    o = accum[h, rows, :] * jnp.exp(old - m) + o
                if end:
                    res.append(o / pltpu.roll(o, 64, 1))
                    if hh:
                        attn[rows, pl.ds(pl.multiple_of(hp * BLOCK, BLOCK), BLOCK)] = jnp.where(
                            low, res[-2], res[-1]
                        ).astype(BF16)
                else:
                    accum[h, rows, :] = o
                    peak[h, rows, :] = jnp.broadcast_to(m, (size, BLOCK))

    lon_copy(1).wait_recv()
    fwd_copy(1).start()
    queries(keys_values(0, 2), 0)
    for n in (1, 2):
        lon_copy(n).wait_send()
    for n in (4, 7, 6):
        lon_copy(n).start()
    lon_copy(2).wait_recv()
    fwd_copy(2).start()
    for n in (0, 1):
        fwd_copy(n).wait_recv()
    keys_values(4, 2)
    lon_copy(3).wait_recv()
    fwd_copy(3).start()
    queries(keys_values(2, 2), 1)
    attend(0, 512, 0, 6, (0, 2), begin=True)
    lon_copy(5).wait_recv()
    fwd_copy(5).start()
    lon_copy(4).wait_recv()
    fwd_copy(4).start()
    attend(0, 512, 0, 6, (2, 4), begin=True)
    for n in (2, 3):
        fwd_copy(n).wait_recv()
    keys_values(6, 4)
    for n in (4, 5):
        fwd_copy(n).wait_recv()
    keys_values(10, 2)
    attend(0, 512, 6, 6, (0, 2))
    for n in (6, 7):
        lon_copy(n).wait_recv()
        fwd_copy(n).start()
    attend(0, 512, 6, 6, (2, 4))
    keys_values(12, 2)
    for n in (6, 7):
        fwd_copy(n).wait_recv()
    keys_values(14, 2)
    loads[1].wait()

    def mer_copy(dr, dy, dl):
        ty, tl = (y + dy) % 4, (zl + dl) % 2
        n = (dr * 4 + dy) * 2 + dl
        src = mixed.at[dr, :, pl.ds(pl.multiple_of((ty * 2 + tl) * 16, 16), 16), :]
        dst = merx.at[piece_at(dr, (4 - dy) % 4, dl)]
        if n == 0:
            return pltpu.make_async_copy(src, dst, l_sem.at[1])
        return pltpu.make_async_remote_copy(
            src_ref=src, dst_ref=dst, send_sem=mer_ss.at[n], recv_sem=mer_rs.at[n],
            device_id=dev(zh, flip_x(dr), c, ty, tl), device_id_type=MESH,
        )

    mer_steps = [(dr, dy, dl) for dr in range(2) for dy, dl in lat_steps]
    for e in (1, 0):
        attend(e * 256, 256, 12, 4, (0, 4), end=True)
        new = dot(attn[e * 256 : (e + 1) * 256, :], lon_out[...])
        for dz in range(2):
            part = rowx[2 * dz + e].astype(F32) + new[dz * BLOCK : (dz + 1) * BLOCK]
            mixed[e, dz] = part.astype(BF16)
        for dy, dl in lat_steps[::-1]:
            mer_copy(e, dy, dl).start()
    for load in loads[2:]:
        load.wait()
    for dr in (1, 0):
        for dy, dl in lat_steps:
            if dr + dy + dl:
                mer_copy(dr, dy, dl).wait_recv()
            else:
                mer_copy(dr, dy, dl).wait()
        parts = [[], []]
        for near in range(2):
            p0 = near * 8 + dr * 4
            cells = merx[p0 : p0 + 4].astype(F32).reshape(8, 2, 8, CH)
            for g in range(2):
                parts[g].append(cells[:, g].reshape(64, CH))
        cells = jnp.concatenate(parts[0] + parts[1], axis=0)
        qkv = dot(rms(cells, mer_gain[...]), mer_qkv[...]).astype(BF16)
        for q in range(4):
            r0 = (q // 2) * 256 + (q % 2) * 128 + dr * 64
            xg[r0 : r0 + 64, :] = cells[q * 64 : (q + 1) * 64]
            for j in range(12):
                mqkv[j, r0 : r0 + 64, :] = qkv[q * 64 : (q + 1) * 64, j * BLOCK : (j + 1) * BLOCK]

    low_256 = lax.broadcasted_iota(jnp.int32, (256, BLOCK), 1) < 64
    none = jnp.zeros((256, BLOCK), BF16)
    ones_256 = jnp.ones((256, BLOCK), BF16)

    @pl.loop(0, 4)
    def _(hp):
        far = dist[...]
        scores = []
        for g in range(2):
            rows = slice(g * 256, (g + 1) * 256)
            qp = mqkv[hp, rows, :] * jnp.bfloat16(0.125)
            both = jnp.concatenate([jnp.where(low_256, qp, none), jnp.where(low_256, none, qp)], axis=0)
            scores.append(dot_nt(both, mqkv[4 + hp, rows, :]))
        for g in range(2):
            rows = slice(g * 256, (g + 1) * 256)
            p = []
            for hh in range(2):
                sc = scores[g][hh * 256 : (hh + 1) * 256]
                sc = jnp.where(far >= 0.0, sc - far * slopes[2 * hp + hh], NEG)
                p.append(jnp.exp(sc - jnp.max(sc, axis=-1, keepdims=True)).astype(BF16))
            values = jnp.concatenate([mqkv[8 + hp, rows, :], ones_256], axis=1)
            o = dot(jnp.concatenate(p, axis=0), values)
            o = o[:, :BLOCK] / o[:, BLOCK:]
            attn[rows, pl.ds(pl.multiple_of(hp * BLOCK, BLOCK), BLOCK)] = jnp.where(
                low_256, o[:256], o[256:]
            ).astype(BF16)

    def out_copy(dz, dy, dl):
        tz, ty, tl = (zh + dz) % 2, (y + dy) % 4, (zl + dl) % 2
        n = (dz * 4 + dy) * 2 + dl
        piece = piece_at(0, dy, dl)
        src = outs.at[piece // 8, :, piece % 4, dz]
        dst = out.at[s, :, pl.ds(pl.multiple_of(band * 16, 16), 16), :]
        if n == 0:
            return pltpu.make_async_copy(src, dst, l_sem.at[2])
        return pltpu.make_async_remote_copy(
            src_ref=src, dst_ref=dst, send_sem=out_ss.at[n], recv_sem=out_rs.at[n],
            device_id=dev(tz, x, c, ty, tl), device_id_type=MESH,
        )

    for near in range(2):
        halves = []
        for g in range(2):
            r0 = g * 256 + near * 128
            halves.append(xg[r0 : r0 + 128, :] + dot(attn[r0 : r0 + 128, :], mer_out[...]))
        mm = jnp.concatenate([h.reshape(16, 1, 8, CH) for h in halves], axis=1).reshape(256, CH)
        mm = mm.astype(BF16).astype(F32)
        normed = rms(mm, mlp_gain[...])

        def up(j):
            return dot(normed, mlp_in[:, j * CH : (j + 1) * CH])

        ahead = up(0)
        for j in range(4):
            hidden = ahead
            if j < 3:
                ahead = up(j + 1)
            mm = mm + dot(jax.nn.gelu(hidden).astype(BF16), mlp_out[j * CH : (j + 1) * CH, :])
        mm = mm.astype(BF16).reshape(2, 4, 2, 16, CH)
        for dr in range(2):
            outs[near, (r + dr) % 2] = mm[dr]
        for dy in ((2, 1), (3, 0))[near]:
            for dz in (1, 0):
                for dl in (1, 0):
                    out_copy(dz, dy, dl).start()

    for n in (3, 4, 5, 6, 7):
        lon_copy(n).wait_send()
    for n in range(8):
        fwd_copy(n).wait_send()
    for step in mer_steps:
        if sum(step):
            mer_copy(*step).wait_send()
    for step in mer_steps:
        out_copy(*step).wait()


def per_device(
    weather, windows, window_table, lon_gain, lon_qkv, lon_out, mer_gain, mer_qkv, mer_out,
    slopes, mlp_gain, mlp_in, mlp_out,
):
    vmem = pl.BlockSpec(memory_space=pltpu.VMEM)
    smem = pl.BlockSpec(memory_space=pltpu.SMEM)
    hbm = pl.BlockSpec(memory_space=pl.ANY)
    dma = pltpu.SemaphoreType.DMA
    return pl.pallas_call(
        kernel,
        out_shape=jax.ShapeDtypeStruct(weather.shape, BF16),
        in_specs=[hbm, smem, smem, vmem, vmem, vmem, smem] + [hbm] * 6,
        out_specs=hbm,
        scratch_shapes=[
            pltpu.VMEM((16, BLOCK, CH), BF16),
            pltpu.VMEM((4, BLOCK, 2048), BF16),
            pltpu.VMEM((8, 2048, BLOCK), BF16),
            pltpu.VMEM((4, 512, BLOCK), BF16),
            pltpu.VMEM((8, 512, BLOCK), F32),
            pltpu.VMEM((8, 512, BLOCK), F32),
            pltpu.VMEM((512, CH), BF16),
            pltpu.VMEM((2, 2, BLOCK, CH), BF16),
            pltpu.VMEM((16, 2, 16, CH), BF16),
            pltpu.VMEM((512, CH), F32),
            pltpu.VMEM((12, 512, BLOCK), BF16),
            pltpu.VMEM((2, 2, 4, 2, 16, CH), BF16),
            pltpu.VMEM((BLOCK, 2048), BF16),
            pltpu.VMEM((256, 256), F32),
            pltpu.VMEM((512, 1536), BF16),
            pltpu.VMEM((512, 512), BF16),
            pltpu.VMEM((512, 1536), BF16),
            pltpu.VMEM((512, 512), BF16),
            pltpu.VMEM((512, 2048), BF16),
            pltpu.VMEM((2048, 512), BF16),
            dma((6,)), dma((3,)),
            dma((8,)), dma((8,)), dma((8,)), dma((8,)),
            dma((16,)), dma((16,)), dma((16,)), dma((16,)),
        ],
        compiler_params=pltpu.CompilerParams(
            collective_id=0, has_side_effects=True, vmem_limit_bytes=56 * 1024 * 1024
        ),
        name="axial",
    )(
        weather, windows, window_table,
        lon_gain.reshape(1, CH), mer_gain.reshape(1, CH), mlp_gain.reshape(1, CH), slopes,
        lon_qkv, lon_out, mer_qkv, mer_out, mlp_in, mlp_out,
    )


def solution(mesh):
    return jax.shard_map(
        per_device,
        mesh=mesh,
        in_specs=(
            P(None, "lat", "lon", None), P("lat"), P("lat", None),
            P(), P(), P(), P(), P(), P(), P(), P(), P(), P(),
        ),
        out_specs=P(None, "lat", "lon", None),
        check_vma=False,
    )
```

```python
import functools

import jax
import jax.numpy as jnp
from jax import lax
from jax.experimental import pallas as pl
from jax.experimental.pallas import tpu as pltpu
from jax.sharding import PartitionSpec as P

MESH = pl.DeviceIdType.MESH
F32 = jnp.float32
BF16 = jnp.bfloat16
BLOCK = 128
CH = 512
NEG = -1e30
EPS = 1e-06


def rms(x, gain):
    inv = lax.rsqrt(jnp.mean(x * x, axis=-1, keepdims=True) + EPS)
    return (x * inv * gain).astype(BF16)


def dot(a, b):
    return jnp.dot(a, b, preferred_element_type=F32)


def dot_nt(a, b):
    return lax.dot_general(a, b, (((1,), (1,)), ((), ())), preferred_element_type=F32)


def kernel(
    weather, windows, table, lon_gain, mer_gain, mlp_gain, slopes,
    lon_qkv_h, lon_out_h, mer_qkv_h, mer_out_h, mlp_in_h, mlp_out_h,
    out,
    rowx, kt, vaug, qs, peak, accum, attn, mixed, merx, xg, mqkv, outs, bias, dist,
    lon_qkv, lon_out, mer_qkv, mer_out, mlp_in, mlp_out,
    w_sem, l_sem, lon_ss, lon_rs, fwd_ss, fwd_rs, mer_ss, mer_rs, out_ss, out_rs,
):
    lo, band = lax.axis_index("lon"), lax.axis_index("lat")
    zh, x, c = lo // 8, (lo // 2) % 4, lo % 2
    y, zl = band // 2, band % 2
    r = x % 2
    s = (x // 2 + zh) % 2

    def dev(zh, x, c, y, zl):
        return ((zh * 4 + x) * 2 + c, y * 2 + zl)

    def flip_x(e):
        return ((x // 2 + e // 2) % 2) * 2 + (x % 2 + e % 2) % 2

    loads = [
        pltpu.make_async_copy(src, dst, w_sem.at[i])
        for i, (src, dst) in enumerate(
            [(lon_qkv_h, lon_qkv), (lon_out_h, lon_out), (mer_qkv_h, mer_qkv),
             (mer_out_h, mer_out), (mlp_in_h, mlp_in), (mlp_out_h, mlp_out)]
        )
    ]
    own_copy = pltpu.make_async_copy(weather.at[s, r], rowx.at[0], l_sem.at[0])
    own_copy.start()
    loads[0].start()

    barrier = pltpu.get_barrier_semaphore()
    peers = [dev((zh + dz) % 2, flip_x(e), c, y, zl) for dz in range(2) for e in range(4) if dz + e]
    peers.append(dev(zh, x, 1 - c, y, zl))
    lat_steps = [(dy, dl) for dy in range(4) for dl in range(2)]
    peers += [
        dev(zh, flip_x(dr), c, (y + dy) % 4, (zl + dl) % 2)
        for dr in range(2) for dy, dl in lat_steps if dy + dl
    ]
    peers += [dev(1 - zh, x, c, (y + dy) % 4, (zl + dl) % 2) for dy, dl in lat_steps if dy + dl]
    for peer in peers:
        pl.semaphore_signal(barrier, inc=1, device_id=peer, device_id_type=MESH)
    pl.semaphore_wait(barrier, len(peers))

    def away(n):
        return (n // 2) % 2, n % 2 + 2 * (n // 4)

    def slot(n, handed):
        return ((4, 8, 10, 14) if handed else (0, 2, 6, 12))[n // 2] + n % 2

    def lon_copy(n):
        dz, e = away(n)
        tz, tx = (zh + dz) % 2, flip_x(e)
        return pltpu.make_async_remote_copy(
            src_ref=weather.at[(tx // 2 + tz) % 2, tx % 2],
            dst_ref=rowx.at[slot(n, False)],
            send_sem=lon_ss.at[n],
            recv_sem=lon_rs.at[n],
            device_id=dev(tz, tx, c, y, zl),
            device_id_type=MESH,
        )

    def fwd_copy(n):
        return pltpu.make_async_remote_copy(
            src_ref=rowx.at[slot(n, False)],
            dst_ref=rowx.at[slot(n, True)],
            send_sem=fwd_ss.at[n],
            recv_sem=fwd_rs.at[n],
            device_id=dev(zh, x, 1 - c, y, zl),
            device_id_type=MESH,
        )

    for n in (2, 1, 3, 5):
        lon_copy(n).start()
    own_copy.wait()
    fwd_copy(0).start()
    for load in loads[1:]:
        load.start()

    width = windows[r]
    rows_128 = lax.broadcasted_iota(jnp.int32, (BLOCK, BLOCK), 0)
    for n in range(8):
        for handed in range(2):
            dz, e = away(n)
            kb = ((zh + dz) % 2) * 8 + flip_x(e) * 2 + (c + handed) % 2
            value = jnp.zeros((BLOCK, BLOCK), F32)
            for qi in range(4):
                qb = ((zh + qi % 2) % 2) * 8 + flip_x(qi // 2) * 2 + c
                d = (kb - qb + 16) % 16
                seen = (jnp.minimum(d, 16 - d) <= width) & ((d == 0) | (table[r, d] == 1))
                value = jnp.where(rows_128 == qi, jnp.where(seen, 0.0, NEG), value)
            k0 = slot(n, handed) * BLOCK
            bias[:, k0 : k0 + BLOCK] = value.astype(BF16)

    def piece_at(dr, dy, dl):
        near = 0 if dy in (1, 2) else 1
        return near * 8 + dr * 4 + ((dy - 1 - 2 * near) % 4) * 2 + dl

    def position(i):
        near, dr, dyi, dl = i // 128, (i // 64) % 2, (i // 32) % 2, (i // 16) % 2
        row = (((y + 1 + 2 * near + dyi) % 4) * 2 + (zl + dl) % 2) * 2 + (r + dr) % 2
        half = ((i // 8) % 2 + zh) % 2
        return jnp.where(half == 0, row, 31 - row)

    ii = lax.broadcasted_iota(jnp.int32, (256, 256), 0)
    jj = lax.broadcasted_iota(jnp.int32, (256, 256), 1)
    apart = jnp.abs(position(ii) - position(jj))
    apart = jnp.minimum(apart, 32 - apart).astype(F32)
    dist[...] = jnp.where(ii % 8 == jj % 8, apart, -1.0)

    loads[0].wait()

    def keys_values(first, count):
        size = count * BLOCK
        normed = rms(rowx[first : first + count].reshape(size, CH).astype(F32), lon_gain[...])
        cells = slice(first * BLOCK, first * BLOCK + size)
        k = dot(normed, lon_qkv[:, CH : 2 * CH])
        kt[:, :, cells] = k.T.astype(BF16).reshape(4, BLOCK, size)
        v = dot(normed, lon_qkv[:, 2 * CH :]).astype(BF16)
        low = lax.broadcasted_iota(jnp.int32, (size, BLOCK), 1) < 64
        one = jnp.ones((size, BLOCK), BF16)
        for hp in range(4):
            part = v[:, hp * BLOCK : (hp + 1) * BLOCK]
            vaug[2 * hp, cells, :] = jnp.where(low, part, one)
            vaug[2 * hp + 1, cells, :] = jnp.where(low, one, part)
        return normed

    def queries(normed, dz):
        q = dot(normed, lon_qkv[:, :CH]).astype(BF16) * jnp.bfloat16(0.125)
        for e in range(2):
            for hp in range(4):
                r0 = (e * 2 + dz) * BLOCK
                qs[hp, r0 : r0 + BLOCK, :] = q[e * BLOCK : (e + 1) * BLOCK, hp * BLOCK : (hp + 1) * BLOCK]

    def attend(r0, size, first, count, heads, begin=False, end=False):
        rows = slice(r0, r0 + size)
        cells = slice(first * BLOCK, (first + count) * BLOCK)
        low = lax.broadcasted_iota(jnp.int32, (size, BLOCK), 1) < 64
        none = jnp.zeros((size, BLOCK), BF16)
        block = lax.broadcasted_iota(jnp.int32, (size, BLOCK), 0) // BLOCK + r0 // BLOCK
        lane = lax.broadcasted_iota(jnp.int32, (size, BLOCK), 1)
        hot = jnp.where(block == lane, 1.0, 0.0).astype(BF16)

        def score(hp, hh):
            qp = qs[hp, rows, :]
            qms = [jnp.where(low, qp, none), jnp.where(low, none, qp)]
            kp = jnp.concatenate([kt[hp, :, cells], bias[:, cells]], axis=0)
            if not end:
                return dot(jnp.concatenate([qms[hh], hot], axis=1), kp)
            if hh == 0:
                both = jnp.concatenate([jnp.concatenate([qm, hot], axis=1) for qm in qms], axis=0)
                stacked.append(dot(both, kp))
            return stacked[-1][hh * size : (hh + 1) * size]

        stacked = []

        @pl.loop(heads[0], heads[1], step=2)
        def _(pair):
            units = [(pair + j, hh) for j in range(2) for hh in range(2)]
            ahead = score(*units[0])
            res = []
            for i, (hp, hh) in enumerate(units):
                sc = ahead
                if i + 1 < len(units):
                    ahead = score(*units[i + 1])
                h = 2 * hp + hh
                m = jnp.max(sc, axis=-1, keepdims=True)
                if begin:
                    p = jnp.exp(sc - m).astype(BF16)
                    o = dot(p, vaug[h, cells, :])
                else:
                    old = peak[h, rows, :]
                    m = jnp.maximum(old, m)
                    p = [jnp.exp(sc[:, j * BLOCK : (j + 1) * BLOCK] - m).astype(BF16) for j in range(count)]
                    o = dot(jnp.concatenate(p, axis=1), vaug[h, cells, :])
                    o = accum[h, rows, :] * jnp.exp(old - m) + o
                if end:
                    res.append(o / pltpu.roll(o, 64, 1))
                    if hh:
                        attn[rows, pl.ds(pl.multiple_of(hp * BLOCK, BLOCK), BLOCK)] = jnp.where(
                            low, res[-2], res[-1]
                        ).astype(BF16)
                else:
                    accum[h, rows, :] = o
                    peak[h, rows, :] = jnp.broadcast_to(m, (size, BLOCK))

    lon_copy(1).wait_recv()
    fwd_copy(1).start()
    queries(keys_values(0, 2), 0)
    for n in (1, 2):
        lon_copy(n).wait_send()
    for n in (4, 7, 6):
        lon_copy(n).start()
    lon_copy(2).wait_recv()
    fwd_copy(2).start()
    for n in (0, 1):
        fwd_copy(n).wait_recv()
    keys_values(4, 2)
    lon_copy(3).wait_recv()
    fwd_copy(3).start()
    queries(keys_values(2, 2), 1)
    attend(0, 512, 0, 6, (0, 2), begin=True)
    lon_copy(5).wait_recv()
    fwd_copy(5).start()
    lon_copy(4).wait_recv()
    fwd_copy(4).start()
    attend(0, 512, 0, 6, (2, 4), begin=True)
    for n in (2, 3):
        fwd_copy(n).wait_recv()
    keys_values(6, 4)
    for n in (4, 5):
        fwd_copy(n).wait_recv()
    keys_values(10, 2)
    attend(0, 512, 6, 6, (0, 2))
    for n in (6, 7):
        lon_copy(n).wait_recv()
        fwd_copy(n).start()
    attend(0, 512, 6, 6, (2, 4))
    keys_values(12, 2)
    for n in (6, 7):
        fwd_copy(n).wait_recv()
    keys_values(14, 2)
    loads[1].wait()

    def mer_copy(dr, dy, dl):
        ty, tl = (y + dy) % 4, (zl + dl) % 2
        n = (dr * 4 + dy) * 2 + dl
        src = mixed.at[dr, :, pl.ds(pl.multiple_of((ty * 2 + tl) * 16, 16), 16), :]
        dst = merx.at[piece_at(dr, (4 - dy) % 4, dl)]
        if n == 0:
            return pltpu.make_async_copy(src, dst, l_sem.at[1])
        return pltpu.make_async_remote_copy(
            src_ref=src, dst_ref=dst, send_sem=mer_ss.at[n], recv_sem=mer_rs.at[n],
            device_id=dev(zh, flip_x(dr), c, ty, tl), device_id_type=MESH,
        )

    mer_steps = [(dr, dy, dl) for dr in range(2) for dy, dl in lat_steps]
    for e in (1, 0):
        attend(e * 256, 256, 12, 4, (0, 4), end=True)
        new = dot(attn[e * 256 : (e + 1) * 256, :], lon_out[...])
        for dz in range(2):
            part = rowx[2 * dz + e].astype(F32) + new[dz * BLOCK : (dz + 1) * BLOCK]
            mixed[e, dz] = part.astype(BF16)
        for dy, dl in lat_steps[::-1]:
            mer_copy(e, dy, dl).start()
    for load in loads[2:]:
        load.wait()
    for dr in (1, 0):
        for dy, dl in lat_steps:
            if dr + dy + dl:
                mer_copy(dr, dy, dl).wait_recv()
            else:
                mer_copy(dr, dy, dl).wait()
        parts = [[], []]
        for near in range(2):
            p0 = near * 8 + dr * 4
            cells = merx[p0 : p0 + 4].astype(F32).reshape(8, 2, 8, CH)
            for g in range(2):
                parts[g].append(cells[:, g].reshape(64, CH))
        cells = jnp.concatenate(parts[0] + parts[1], axis=0)
        qkv = dot(rms(cells, mer_gain[...]), mer_qkv[...]).astype(BF16)
        for q in range(4):
            r0 = (q // 2) * 256 + (q % 2) * 128 + dr * 64
            xg[r0 : r0 + 64, :] = cells[q * 64 : (q + 1) * 64]
            for j in range(12):
                mqkv[j, r0 : r0 + 64, :] = qkv[q * 64 : (q + 1) * 64, j * BLOCK : (j + 1) * BLOCK]

    low_128 = lax.broadcasted_iota(jnp.int32, (BLOCK, BLOCK), 1) < 64
    none = jnp.zeros((BLOCK, BLOCK), BF16)
    ones_256 = jnp.ones((256, BLOCK), BF16)

    def out_copy(dz, dy, dl):
        tz, ty, tl = (zh + dz) % 2, (y + dy) % 4, (zl + dl) % 2
        n = (dz * 4 + dy) * 2 + dl
        piece = piece_at(0, dy, dl)
        src = outs.at[piece // 8, :, piece % 4, dz]
        dst = out.at[s, :, pl.ds(pl.multiple_of(band * 16, 16), 16), :]
        if n == 0:
            return pltpu.make_async_copy(src, dst, l_sem.at[2])
        return pltpu.make_async_remote_copy(
            src_ref=src, dst_ref=dst, send_sem=out_ss.at[n], recv_sem=out_rs.at[n],
            device_id=dev(tz, x, c, ty, tl), device_id_type=MESH,
        )

    for near in range(2):
        @pl.loop(0, 4, step=4)
        def _(hp0):
            far = dist[near * 128 : near * 128 + 128, :]
            units = [(hp0 + j, g) for j in range(4) for g in range(2)]
            scores = []
            for hp, g in units:
                qp = mqkv[hp, g * 256 + near * 128 : g * 256 + near * 128 + 128, :] * jnp.bfloat16(0.125)
                both = jnp.concatenate([jnp.where(low_128, qp, none), jnp.where(low_128, none, qp)], axis=0)
                scores.append(dot_nt(both, mqkv[4 + hp, g * 256 : (g + 1) * 256, :]))
            for (hp, g), both in zip(units, scores):
                p = []
                for hh in range(2):
                    sc = both[hh * 128 : (hh + 1) * 128]
                    sc = jnp.where(far >= 0.0, sc - far * slopes[2 * hp + hh], NEG)
                    p.append(jnp.exp(sc - jnp.max(sc, axis=-1, keepdims=True)).astype(BF16))
                values = jnp.concatenate([mqkv[8 + hp, g * 256 : (g + 1) * 256, :], ones_256], axis=1)
                o = dot(jnp.concatenate(p, axis=0), values)
                o = o[:, :BLOCK] / o[:, BLOCK:]
                rows = slice(g * 256 + near * 128, g * 256 + near * 128 + 128)
                attn[rows, pl.ds(pl.multiple_of(hp * BLOCK, BLOCK), BLOCK)] = jnp.where(
                    low_128, o[:128], o[128:]
                ).astype(BF16)

        halves = []
        for g in range(2):
            r0 = g * 256 + near * 128
            halves.append(xg[r0 : r0 + 128, :] + dot(attn[r0 : r0 + 128, :], mer_out[...]))
        mm = jnp.concatenate([h.reshape(16, 1, 8, CH) for h in halves], axis=1).reshape(256, CH)
        mm = mm.astype(BF16).astype(F32)
        normed = rms(mm, mlp_gain[...])

        def up(j):
            return dot(normed, mlp_in[:, j * CH : (j + 1) * CH])

        ahead = up(0)
        for j in range(4):
            hidden = ahead
            if j < 3:
                ahead = up(j + 1)
            mm = mm + dot(jax.nn.gelu(hidden).astype(BF16), mlp_out[j * CH : (j + 1) * CH, :])
        mm = mm.astype(BF16).reshape(2, 4, 2, 16, CH)
        for dr in range(2):
            outs[near, (r + dr) % 2] = mm[dr]
        for dy in ((2, 1), (3, 0))[near]:
            for dz in (1, 0):
                for dl in (1, 0):
                    out_copy(dz, dy, dl).start()

    for n in (3, 4, 5, 6, 7):
        lon_copy(n).wait_send()
    for n in range(8):
        fwd_copy(n).wait_send()
    for step in mer_steps:
        if sum(step):
            mer_copy(*step).wait_send()
    for step in mer_steps:
        out_copy(*step).wait()


def per_device(
    weather, windows, window_table, lon_gain, lon_qkv, lon_out, mer_gain, mer_qkv, mer_out,
    slopes, mlp_gain, mlp_in, mlp_out,
):
    vmem = pl.BlockSpec(memory_space=pltpu.VMEM)
    smem = pl.BlockSpec(memory_space=pltpu.SMEM)
    hbm = pl.BlockSpec(memory_space=pl.ANY)
    dma = pltpu.SemaphoreType.DMA
    return pl.pallas_call(
        kernel,
        out_shape=jax.ShapeDtypeStruct(weather.shape, BF16),
        in_specs=[hbm, smem, smem, vmem, vmem, vmem, smem] + [hbm] * 6,
        out_specs=hbm,
        scratch_shapes=[
            pltpu.VMEM((16, BLOCK, CH), BF16),
            pltpu.VMEM((4, BLOCK, 2048), BF16),
            pltpu.VMEM((8, 2048, BLOCK), BF16),
            pltpu.VMEM((4, 512, BLOCK), BF16),
            pltpu.VMEM((8, 512, BLOCK), F32),
            pltpu.VMEM((8, 512, BLOCK), F32),
            pltpu.VMEM((512, CH), BF16),
            pltpu.VMEM((2, 2, BLOCK, CH), BF16),
            pltpu.VMEM((16, 2, 16, CH), BF16),
            pltpu.VMEM((512, CH), F32),
            pltpu.VMEM((12, 512, BLOCK), BF16),
            pltpu.VMEM((2, 2, 4, 2, 16, CH), BF16),
            pltpu.VMEM((BLOCK, 2048), BF16),
            pltpu.VMEM((256, 256), F32),
            pltpu.VMEM((512, 1536), BF16),
            pltpu.VMEM((512, 512), BF16),
            pltpu.VMEM((512, 1536), BF16),
            pltpu.VMEM((512, 512), BF16),
            pltpu.VMEM((512, 2048), BF16),
            pltpu.VMEM((2048, 512), BF16),
            dma((6,)), dma((3,)),
            dma((8,)), dma((8,)), dma((8,)), dma((8,)),
            dma((16,)), dma((16,)), dma((16,)), dma((16,)),
        ],
        compiler_params=pltpu.CompilerParams(
            collective_id=0, has_side_effects=True, vmem_limit_bytes=56 * 1024 * 1024
        ),
        name="axial",
    )(
        weather, windows, window_table,
        lon_gain.reshape(1, CH), mer_gain.reshape(1, CH), mlp_gain.reshape(1, CH), slopes,
        lon_qkv, lon_out, mer_qkv, mer_out, mlp_in, mlp_out,
    )


def solution(mesh):
    return jax.shard_map(
        per_device,
        mesh=mesh,
        in_specs=(
            P(None, "lat", "lon", None), P("lat"), P("lat", None),
            P(), P(), P(), P(), P(), P(), P(), P(), P(), P(),
        ),
        out_specs=P(None, "lat", "lon", None),
        check_vma=False,
    )
```

```python
import functools

import jax
import jax.numpy as jnp
from jax import lax
from jax.experimental import pallas as pl
from jax.experimental.pallas import tpu as pltpu
from jax.sharding import PartitionSpec as P

MESH = pl.DeviceIdType.MESH
F32 = jnp.float32
BF16 = jnp.bfloat16
BLOCK = 128
CH = 512
NEG = -1e30
EPS = 1e-06


def rms(x, gain):
    inv = lax.rsqrt(jnp.mean(x * x, axis=-1, keepdims=True) + EPS)
    return (x * inv * gain).astype(BF16)


def dot(a, b):
    return jnp.dot(a, b, preferred_element_type=F32)


def dot_nt(a, b):
    return lax.dot_general(a, b, (((1,), (1,)), ((), ())), preferred_element_type=F32)


def kernel(
    weather, windows, table, lon_gain, mer_gain, mlp_gain, slopes,
    lon_qkv_h, lon_out_h, mer_qkv_h, mer_out_h, mlp_in_h, mlp_out_h,
    out,
    rowx, kt, vaug, qs, peak, accum, attn, mixed, merx, xg, mqkv, outs, bias, dist,
    lon_qkv, lon_out, mer_qkv, mer_out, mlp_in, mlp_out,
    w_sem, l_sem, lon_ss, lon_rs, fwd_ss, fwd_rs, mer_ss, mer_rs, out_ss, out_rs,
):
    lo, band = lax.axis_index("lon"), lax.axis_index("lat")
    zh, x, c = lo // 8, (lo // 2) % 4, lo % 2
    y, zl = band // 2, band % 2
    r = x % 2
    s = (x // 2 + zh) % 2

    def dev(zh, x, c, y, zl):
        return ((zh * 4 + x) * 2 + c, y * 2 + zl)

    def flip_x(e):
        return ((x // 2 + e // 2) % 2) * 2 + (x % 2 + e % 2) % 2

    loads = [
        pltpu.make_async_copy(src, dst, w_sem.at[i])
        for i, (src, dst) in enumerate(
            [(lon_qkv_h, lon_qkv), (lon_out_h, lon_out), (mer_qkv_h, mer_qkv),
             (mer_out_h, mer_out), (mlp_in_h, mlp_in), (mlp_out_h, mlp_out)]
        )
    ]
    own_copy = pltpu.make_async_copy(weather.at[s, r], rowx.at[0], l_sem.at[0])
    own_copy.start()
    loads[0].start()

    barrier = pltpu.get_barrier_semaphore()
    peers = [dev((zh + dz) % 2, flip_x(e), c, y, zl) for dz in range(2) for e in range(4) if dz + e]
    peers.append(dev(zh, x, 1 - c, y, zl))
    lat_steps = [(dy, dl) for dy in range(4) for dl in range(2)]
    peers += [
        dev(zh, flip_x(dr), c, (y + dy) % 4, (zl + dl) % 2)
        for dr in range(2) for dy, dl in lat_steps if dy + dl
    ]
    peers += [dev(1 - zh, x, c, (y + dy) % 4, (zl + dl) % 2) for dy, dl in lat_steps if dy + dl]
    for peer in peers:
        pl.semaphore_signal(barrier, inc=1, device_id=peer, device_id_type=MESH)
    pl.semaphore_wait(barrier, len(peers))

    def away(n):
        return (n // 2) % 2, n % 2 + 2 * (n // 4)

    def slot(n, handed):
        return ((4, 8, 10, 14) if handed else (0, 2, 6, 12))[n // 2] + n % 2

    def lon_copy(n):
        dz, e = away(n)
        tz, tx = (zh + dz) % 2, flip_x(e)
        return pltpu.make_async_remote_copy(
            src_ref=weather.at[(tx // 2 + tz) % 2, tx % 2],
            dst_ref=rowx.at[slot(n, False)],
            send_sem=lon_ss.at[n],
            recv_sem=lon_rs.at[n],
            device_id=dev(tz, tx, c, y, zl),
            device_id_type=MESH,
        )

    def fwd_copy(n):
        return pltpu.make_async_remote_copy(
            src_ref=rowx.at[slot(n, False)],
            dst_ref=rowx.at[slot(n, True)],
            send_sem=fwd_ss.at[n],
            recv_sem=fwd_rs.at[n],
            device_id=dev(zh, x, 1 - c, y, zl),
            device_id_type=MESH,
        )

    for n in (2, 1, 3, 5):
        lon_copy(n).start()
    own_copy.wait()
    fwd_copy(0).start()
    for load in loads[1:]:
        load.start()

    width = windows[r]
    rows_128 = lax.broadcasted_iota(jnp.int32, (BLOCK, BLOCK), 0)
    for n in range(8):
        for handed in range(2):
            dz, e = away(n)
            kb = ((zh + dz) % 2) * 8 + flip_x(e) * 2 + (c + handed) % 2
            value = jnp.zeros((BLOCK, BLOCK), F32)
            for qi in range(4):
                qb = ((zh + qi % 2) % 2) * 8 + flip_x(qi // 2) * 2 + c
                d = (kb - qb + 16) % 16
                seen = (jnp.minimum(d, 16 - d) <= width) & ((d == 0) | (table[r, d] == 1))
                value = jnp.where(rows_128 == qi, jnp.where(seen, 0.0, NEG), value)
            k0 = slot(n, handed) * BLOCK
            bias[:, k0 : k0 + BLOCK] = value.astype(BF16)

    def piece_at(dr, dy, dl):
        near = 0 if dy in (1, 2) else 1
        return near * 8 + dr * 4 + ((dy - 1 - 2 * near) % 4) * 2 + dl

    def position(i):
        near, dr, dyi, dl = i // 128, (i // 64) % 2, (i // 32) % 2, (i // 16) % 2
        row = (((y + 1 + 2 * near + dyi) % 4) * 2 + (zl + dl) % 2) * 2 + (r + dr) % 2
        half = ((i // 8) % 2 + zh) % 2
        return jnp.where(half == 0, row, 31 - row)

    ii = lax.broadcasted_iota(jnp.int32, (256, 256), 0)
    jj = lax.broadcasted_iota(jnp.int32, (256, 256), 1)
    apart = jnp.abs(position(ii) - position(jj))
    apart = jnp.minimum(apart, 32 - apart).astype(F32)
    dist[...] = jnp.where(ii % 8 == jj % 8, apart, -1.0)

    loads[0].wait()

    def keys_values(first, count):
        size = count * BLOCK
        normed = rms(rowx[first : first + count].reshape(size, CH).astype(F32), lon_gain[...])
        cells = slice(first * BLOCK, first * BLOCK + size)
        k = dot(normed, lon_qkv[:, CH : 2 * CH])
        kt[:, :, cells] = k.T.astype(BF16).reshape(4, BLOCK, size)
        v = dot(normed, lon_qkv[:, 2 * CH :]).astype(BF16)
        low = lax.broadcasted_iota(jnp.int32, (size, BLOCK), 1) < 64
        one = jnp.ones((size, BLOCK), BF16)
        for hp in range(4):
            part = v[:, hp * BLOCK : (hp + 1) * BLOCK]
            vaug[2 * hp, cells, :] = jnp.where(low, part, one)
            vaug[2 * hp + 1, cells, :] = jnp.where(low, one, part)
        return normed

    def queries(normed, dz):
        q = dot(normed, lon_qkv[:, :CH]).astype(BF16) * jnp.bfloat16(0.125)
        for e in range(2):
            for hp in range(4):
                r0 = (e * 2 + dz) * BLOCK
                qs[hp, r0 : r0 + BLOCK, :] = q[e * BLOCK : (e + 1) * BLOCK, hp * BLOCK : (hp + 1) * BLOCK]

    def attend(r0, size, first, count, heads, begin=False, end=False):
        rows = slice(r0, r0 + size)
        cells = slice(first * BLOCK, (first + count) * BLOCK)
        low = lax.broadcasted_iota(jnp.int32, (size, BLOCK), 1) < 64
        none = jnp.zeros((size, BLOCK), BF16)
        block = lax.broadcasted_iota(jnp.int32, (size, BLOCK), 0) // BLOCK + r0 // BLOCK
        lane = lax.broadcasted_iota(jnp.int32, (size, BLOCK), 1)
        hot = jnp.where(block == lane, 1.0, 0.0).astype(BF16)

        def score(hp, hh):
            qp = qs[hp, rows, :]
            qms = [jnp.where(low, qp, none), jnp.where(low, none, qp)]
            kp = jnp.concatenate([kt[hp, :, cells], bias[:, cells]], axis=0)
            if not end:
                return dot(jnp.concatenate([qms[hh], hot], axis=1), kp)
            if hh == 0:
                both = jnp.concatenate([jnp.concatenate([qm, hot], axis=1) for qm in qms], axis=0)
                stacked.append(dot(both, kp))
            return stacked[-1][hh * size : (hh + 1) * size]

        stacked = []

        @pl.loop(heads[0], heads[1], step=2)
        def _(pair):
            units = [(pair + j, hh) for j in range(2) for hh in range(2)]
            ahead = score(*units[0])
            res = []
            for i, (hp, hh) in enumerate(units):
                sc = ahead
                if i + 1 < len(units):
                    ahead = score(*units[i + 1])
                h = 2 * hp + hh
                m = jnp.max(sc, axis=-1, keepdims=True)
                if begin:
                    p = jnp.exp(sc - m).astype(BF16)
                    o = dot(p, vaug[h, cells, :])
                else:
                    old = peak[h, rows, :]
                    m = jnp.maximum(old, m)
                    p = [jnp.exp(sc[:, j * BLOCK : (j + 1) * BLOCK] - m).astype(BF16) for j in range(count)]
                    o = dot(jnp.concatenate(p, axis=1), vaug[h, cells, :])
                    o = accum[h, rows, :] * jnp.exp(old - m) + o
                if end:
                    res.append(o)
                    if hh:
                        attn[rows, pl.ds(pl.multiple_of(hp * BLOCK, BLOCK), BLOCK)] = (
                            jnp.where(low, res[-2], res[-1])
                            / pltpu.roll(jnp.where(low, res[-1], res[-2]), 64, 1)
                        ).astype(BF16)
                else:
                    accum[h, rows, :] = o
                    peak[h, rows, :] = jnp.broadcast_to(m, (size, BLOCK))

    lon_copy(1).wait_recv()
    fwd_copy(1).start()
    queries(keys_values(0, 2), 0)
    for n in (1, 2):
        lon_copy(n).wait_send()
    for n in (4, 7, 6):
        lon_copy(n).start()
    lon_copy(2).wait_recv()
    fwd_copy(2).start()
    for n in (0, 1):
        fwd_copy(n).wait_recv()
    keys_values(4, 2)
    lon_copy(3).wait_recv()
    fwd_copy(3).start()
    queries(keys_values(2, 2), 1)
    attend(0, 512, 0, 6, (0, 2), begin=True)
    lon_copy(5).wait_recv()
    fwd_copy(5).start()
    lon_copy(4).wait_recv()
    fwd_copy(4).start()
    attend(0, 512, 0, 6, (2, 4), begin=True)
    for n in (2, 3):
        fwd_copy(n).wait_recv()
    keys_values(6, 4)
    for n in (4, 5):
        fwd_copy(n).wait_recv()
    keys_values(10, 2)
    attend(0, 512, 6, 6, (0, 2))
    for n in (6, 7):
        lon_copy(n).wait_recv()
        fwd_copy(n).start()
    attend(0, 512, 6, 6, (2, 4))
    keys_values(12, 2)
    for n in (6, 7):
        fwd_copy(n).wait_recv()
    keys_values(14, 2)
    loads[1].wait()

    def mer_copy(dr, dy, dl):
        ty, tl = (y + dy) % 4, (zl + dl) % 2
        n = (dr * 4 + dy) * 2 + dl
        src = mixed.at[dr, :, pl.ds(pl.multiple_of((ty * 2 + tl) * 16, 16), 16), :]
        dst = merx.at[piece_at(dr, (4 - dy) % 4, dl)]
        if n == 0:
            return pltpu.make_async_copy(src, dst, l_sem.at[1])
        return pltpu.make_async_remote_copy(
            src_ref=src, dst_ref=dst, send_sem=mer_ss.at[n], recv_sem=mer_rs.at[n],
            device_id=dev(zh, flip_x(dr), c, ty, tl), device_id_type=MESH,
        )

    mer_steps = [(dr, dy, dl) for dr in range(2) for dy, dl in lat_steps]
    for e in (1, 0):
        attend(e * 256, 256, 12, 4, (0, 4), end=True)
        new = dot(attn[e * 256 : (e + 1) * 256, :], lon_out[...])
        for dz in range(2):
            part = rowx[2 * dz + e].astype(F32) + new[dz * BLOCK : (dz + 1) * BLOCK]
            mixed[e, dz] = part.astype(BF16)
        for dy, dl in lat_steps[::-1]:
            mer_copy(e, dy, dl).start()
    for load in loads[2:]:
        load.wait()
    for dr in (1, 0):
        for dy, dl in lat_steps:
            if dr + dy + dl:
                mer_copy(dr, dy, dl).wait_recv()
            else:
                mer_copy(dr, dy, dl).wait()
        parts = [[], []]
        for near in range(2):
            p0 = near * 8 + dr * 4
            cells = merx[p0 : p0 + 4].astype(F32).reshape(8, 2, 8, CH)
            for g in range(2):
                parts[g].append(cells[:, g].reshape(64, CH))
        cells = jnp.concatenate(parts[0] + parts[1], axis=0)
        qkv = dot(rms(cells, mer_gain[...]), mer_qkv[...]).astype(BF16)
        for q in range(4):
            r0 = (q // 2) * 256 + (q % 2) * 128 + dr * 64
            xg[r0 : r0 + 64, :] = cells[q * 64 : (q + 1) * 64]
            for j in range(12):
                mqkv[j, r0 : r0 + 64, :] = qkv[q * 64 : (q + 1) * 64, j * BLOCK : (j + 1) * BLOCK]

    low_128 = lax.broadcasted_iota(jnp.int32, (BLOCK, BLOCK), 1) < 64
    none = jnp.zeros((BLOCK, BLOCK), BF16)
    ones_256 = jnp.ones((256, BLOCK), BF16)

    def out_copy(dz, dy, dl):
        tz, ty, tl = (zh + dz) % 2, (y + dy) % 4, (zl + dl) % 2
        n = (dz * 4 + dy) * 2 + dl
        piece = piece_at(0, dy, dl)
        src = outs.at[piece // 8, :, piece % 4, dz]
        dst = out.at[s, :, pl.ds(pl.multiple_of(band * 16, 16), 16), :]
        if n == 0:
            return pltpu.make_async_copy(src, dst, l_sem.at[2])
        return pltpu.make_async_remote_copy(
            src_ref=src, dst_ref=dst, send_sem=out_ss.at[n], recv_sem=out_rs.at[n],
            device_id=dev(tz, x, c, ty, tl), device_id_type=MESH,
        )

    for near in range(2):
        @pl.loop(0, 4, step=4)
        def _(hp0):
            far = dist[near * 128 : near * 128 + 128, :]
            units = [(hp0 + j, g) for j in range(4) for g in range(2)]
            scores = []
            for hp, g in units:
                qp = mqkv[hp, g * 256 + near * 128 : g * 256 + near * 128 + 128, :] * jnp.bfloat16(0.125)
                both = jnp.concatenate([jnp.where(low_128, qp, none), jnp.where(low_128, none, qp)], axis=0)
                scores.append(dot_nt(both, mqkv[4 + hp, g * 256 : (g + 1) * 256, :]))
            for (hp, g), both in zip(units, scores):
                p = []
                for hh in range(2):
                    sc = both[hh * 128 : (hh + 1) * 128]
                    sc = jnp.where(far >= 0.0, sc - far * slopes[2 * hp + hh], NEG)
                    p.append(jnp.exp(sc - jnp.max(sc, axis=-1, keepdims=True)).astype(BF16))
                values = jnp.concatenate([mqkv[8 + hp, g * 256 : (g + 1) * 256, :], ones_256], axis=1)
                o = dot(jnp.concatenate(p, axis=0), values)
                total = jnp.where(low_128, o[:128, BLOCK:], o[128:, BLOCK:])
                rows = slice(g * 256 + near * 128, g * 256 + near * 128 + 128)
                attn[rows, pl.ds(pl.multiple_of(hp * BLOCK, BLOCK), BLOCK)] = (
                    jnp.where(low_128, o[:128, :BLOCK], o[128:, :BLOCK]) / total
                ).astype(BF16)

        halves = []
        for g in range(2):
            r0 = g * 256 + near * 128
            halves.append(xg[r0 : r0 + 128, :] + dot(attn[r0 : r0 + 128, :], mer_out[...]))
        mm = jnp.concatenate([h.reshape(16, 1, 8, CH) for h in halves], axis=1).reshape(256, CH)
        mm = mm.astype(BF16).astype(F32)
        normed = rms(mm, mlp_gain[...])

        def up(j):
            return dot(normed, mlp_in[:, j * CH : (j + 1) * CH])

        ahead = up(0)
        for j in range(4):
            hidden = ahead
            if j < 3:
                ahead = up(j + 1)
            mm = mm + dot(jax.nn.gelu(hidden).astype(BF16), mlp_out[j * CH : (j + 1) * CH, :])
        mm = mm.astype(BF16).reshape(2, 4, 2, 16, CH)
        for dr in range(2):
            outs[near, (r + dr) % 2] = mm[dr]
        for dy in ((2, 1), (3, 0))[near]:
            for dz in (1, 0):
                for dl in (1, 0):
                    out_copy(dz, dy, dl).start()

    for n in (3, 4, 5, 6, 7):
        lon_copy(n).wait_send()
    for n in range(8):
        fwd_copy(n).wait_send()
    for step in mer_steps:
        if sum(step):
            mer_copy(*step).wait_send()
    for step in mer_steps:
        out_copy(*step).wait()


def per_device(
    weather, windows, window_table, lon_gain, lon_qkv, lon_out, mer_gain, mer_qkv, mer_out,
    slopes, mlp_gain, mlp_in, mlp_out,
):
    vmem = pl.BlockSpec(memory_space=pltpu.VMEM)
    smem = pl.BlockSpec(memory_space=pltpu.SMEM)
    hbm = pl.BlockSpec(memory_space=pl.ANY)
    dma = pltpu.SemaphoreType.DMA
    return pl.pallas_call(
        kernel,
        out_shape=jax.ShapeDtypeStruct(weather.shape, BF16),
        in_specs=[hbm, smem, smem, vmem, vmem, vmem, smem] + [hbm] * 6,
        out_specs=hbm,
        scratch_shapes=[
            pltpu.VMEM((16, BLOCK, CH), BF16),
            pltpu.VMEM((4, BLOCK, 2048), BF16),
            pltpu.VMEM((8, 2048, BLOCK), BF16),
            pltpu.VMEM((4, 512, BLOCK), BF16),
            pltpu.VMEM((8, 512, BLOCK), F32),
            pltpu.VMEM((8, 512, BLOCK), F32),
            pltpu.VMEM((512, CH), BF16),
            pltpu.VMEM((2, 2, BLOCK, CH), BF16),
            pltpu.VMEM((16, 2, 16, CH), BF16),
            pltpu.VMEM((512, CH), F32),
            pltpu.VMEM((12, 512, BLOCK), BF16),
            pltpu.VMEM((2, 2, 4, 2, 16, CH), BF16),
            pltpu.VMEM((BLOCK, 2048), BF16),
            pltpu.VMEM((256, 256), F32),
            pltpu.VMEM((512, 1536), BF16),
            pltpu.VMEM((512, 512), BF16),
            pltpu.VMEM((512, 1536), BF16),
            pltpu.VMEM((512, 512), BF16),
            pltpu.VMEM((512, 2048), BF16),
            pltpu.VMEM((2048, 512), BF16),
            dma((6,)), dma((3,)),
            dma((8,)), dma((8,)), dma((8,)), dma((8,)),
            dma((16,)), dma((16,)), dma((16,)), dma((16,)),
        ],
        compiler_params=pltpu.CompilerParams(
            collective_id=0, has_side_effects=True, vmem_limit_bytes=56 * 1024 * 1024
        ),
        name="axial",
    )(
        weather, windows, window_table,
        lon_gain.reshape(1, CH), mer_gain.reshape(1, CH), mlp_gain.reshape(1, CH), slopes,
        lon_qkv, lon_out, mer_qkv, mer_out, mlp_in, mlp_out,
    )


def solution(mesh):
    return jax.shard_map(
        per_device,
        mesh=mesh,
        in_specs=(
            P(None, "lat", "lon", None), P("lat"), P("lat", None),
            P(), P(), P(), P(), P(), P(), P(), P(), P(), P(),
        ),
        out_specs=P(None, "lat", "lon", None),
        check_vma=False,
    )
```
